128 devices in a mesh: dp: 8 (over y_lo, z), ctx: 4 (over x), tensor: 4 (over y_hi, core).
Axes of the slice: x: 4, y: 4 (y_hi: 2, y_lo: 2; y = y_hi * 2 + y_lo), z: 4, core: 2. Of those that a mesh axis runs over, the one named last changes fastest.
Arguments:
- hidden_in: bfloat16 [8, 1024, 1024], P('dp', 'ctx'), may hold values from -6 to 6
- segments: int32 [8, 1024], P('dp'), may hold values from 0 to 2, as said below
- cotangent: float32 [8, 1024, 1024], P('dp', 'ctx'), may hold values from -6 to 6
- norm_attn: bfloat16 [2, 1024], replicated, may hold values from 0.5 to 1.5
- w_zx: bfloat16 [2, 1024, 2, 1536], P(None, None, None, 'tensor'), may hold values from -0.1875 to 0.1875
- w_dt: bfloat16 [2, 1024, 24], P(None, None, 'tensor'), may hold values from -0.1875 to 0.1875
- w_bc: bfloat16 [2, 1024, 256], replicated, may hold values from -0.1875 to 0.1875
- conv_x: bfloat16 [2, 1536, 4], P(None, 'tensor'), may hold values from -3 to 3
- conv_bc: bfloat16 [2, 256, 4], replicated, may hold values from -3 to 3
- dt_bias: float32 [2, 24], P(None, 'tensor'), may hold values from -4 to -2
- a_log: float32 [2, 24], P(None, 'tensor'), may hold values from -3 to 0.5
- d_skip: float32 [2, 24], P(None, 'tensor'), may hold values from 0.5 to 1.5
- w_q: bfloat16 [2, 1024, 512], P(None, None, 'tensor'), may hold values from -0.1875 to 0.1875
- w_kv: bfloat16 [2, 1024, 2, 128], replicated, may hold values from -0.1875 to 0.1875
- w_o: bfloat16 [2, 1024, 512], P(None, None, 'tensor'), may hold values from -1 to 1
- w_out: bfloat16 [2, 1024, 1536], P(None, None, 'tensor'), may hold values from -0.15625 to 0.15625
- norm_ffn: bfloat16 [2, 1024], replicated, may hold values from 0.5 to 1.5
- w_gu: bfloat16 [2, 1024, 2, 2048], P(None, None, None, 'tensor'), may hold values from -0.1875 to 0.1875
- w_down: bfloat16 [2, 1024, 2048], P(None, None, 'tensor'), may hold values from -0.125 to 0.125
Outputs:
- out: bfloat16 [8, 1024, 1024], P('dp', 'ctx')
- grad_hidden_in: float32 [8, 1024, 1024], P('dp', 'ctx')
- grad_norm_attn: float32 [2, 1024], P(None, ('dp', 'ctx', 'tensor'))
- grad_w_zx: float32 [2, 1024, 2, 1536], P(None, ('dp', 'ctx'), None, 'tensor')
- grad_w_dt: float32 [2, 1024, 24], P(None, ('dp', 'ctx'), 'tensor')
- grad_w_bc: float32 [2, 1024, 256], P(None, ('dp', 'ctx', 'tensor'))
- grad_conv_x: float32 [2, 1536, 4], P(None, 'tensor')
- grad_conv_bc: float32 [2, 256, 4], P(None, ('dp', 'ctx', 'tensor'))
- grad_dt_bias: float32 [2, 24], P(None, 'tensor')
- grad_a_log: float32 [2, 24], P(None, 'tensor')
- grad_d_skip: float32 [2, 24], P(None, 'tensor')
- grad_w_q: float32 [2, 1024, 512], P(None, ('dp', 'ctx'), 'tensor')
- grad_w_kv: float32 [2, 1024, 2, 128], P(None, ('dp', 'ctx', 'tensor'))
- grad_w_o: float32 [2, 1024, 512], P(None, ('dp', 'ctx'), 'tensor')
- grad_w_out: float32 [2, 1024, 1536], P(None, ('dp', 'ctx'), 'tensor')
- grad_norm_ffn: float32 [2, 1024], P(None, ('dp', 'ctx', 'tensor'))
- grad_w_gu: float32 [2, 1024, 2, 2048], P(None, ('dp', 'ctx'), None, 'tensor')
- grad_w_down: float32 [2, 1024, 2048], P(None, ('dp', 'ctx'), 'tensor')
The draws below stay inside these ranges and needn't reach their ends.
Inputs may be any that keep to these rules, and one draw needn't show every extreme that they name: `segments`: segment numbers start at 0 and never fall along a sequence; every document holds at least 128 tokens. In every sequence one document covers the positions 255 to 768.
All inputs are finite; a program needn't handle non-finite values.
Results may differ from the reference program's by a relative error of at most 0.035.
Values may be sent and summed in bfloat16 or wider, within the bound.
No kernel may reach another device: no remote copies, remote signals or barrier semaphores. Data moves between devices by JAX's collectives and lax.ppermute only.
A program may use at most 192 MiB of HBM per device.

```python
import jax
import jax.numpy as jnp
from jax import lax

D = 1024
HM = 24
HP = 64
NS = 128
HQ = 8
HK = 2
HD = 64
FF = 2048
LAYERS = 2
LEN = 1024
SEQS = 8
MIN_DOC = 128


def draw_segments(key, part):
    key = jax.random.fold_in(key, 5)
    key_one, key_two, key_three, key_four = jax.random.split(key, 4)
    first_end = jax.random.randint(key_one, (SEQS, 1), MIN_DOC, LEN // 4)
    last_start = jax.random.randint(key_two, (SEQS, 1), LEN - LEN // 4 + 1, LEN - MIN_DOC + 1)
    row_ids = jnp.arange(SEQS, dtype=jnp.int32)[:, None]
    use_first = (jax.random.randint(key_three, (SEQS, 1), 0, 2) == 1) | (row_ids == 0)
    use_last = (jax.random.randint(key_four, (SEQS, 1), 0, 2) == 1) | (row_ids == 0)
    positions = jnp.arange(LEN, dtype=jnp.int32)[None, :]
    return ((positions >= first_end) & use_first).astype(jnp.int32) + ((positions >= last_start) & use_last).astype(jnp.int32)


def steps_of(key, dims, cuts, low, largest):
    gain, own = 1.0, jax.random.fold_in(key, 6)
    for axis_at, parts in cuts:
        heights = jnp.exp(jax.random.uniform(jax.random.fold_in(own, axis_at), (parts,), jnp.float32, low / len(cuts), largest / len(cuts)))
        gain = gain * jnp.repeat(heights, dims[axis_at] // parts).reshape([-1 if axis == axis_at else 1 for axis in range(len(dims))])
    return gain


def gaussian(key, dims, width, reach, cuts=(), kind=jnp.bfloat16):
    values = jax.random.normal(key, dims, jnp.float32) * width
    if len(cuts) > 0:
        values = steps_of(key, dims, cuts, -0.22, 0.18) * values
    return jnp.clip(values, min=-reach, max=reach).astype(kind)


def setup_inputs(seed: int = 0) -> dict:
    arg_keys = jax.random.split(jax.random.key(seed), 20)
    hidden_in = gaussian(arg_keys[0], (SEQS, LEN, D), 1.0, 6.0, ((0, 8), (1, 4)))
    segments = draw_segments(jax.random.fold_in(arg_keys[19], 71), 0)
    cotangent = gaussian(arg_keys[2], (SEQS, LEN, D), 1.0, 6.0, ((0, 8), (1, 4)), jnp.float32)
    norm_attn = jnp.clip(1.0 + 0.1 * jax.random.normal(arg_keys[3], (LAYERS, D), jnp.float32), 0.5, 1.5).astype(jnp.bfloat16)
    w_zx = gaussian(arg_keys[4], (LAYERS, D, 2, HM * HP), D ** -0.5, 0.1875, ((3, 4),))
    w_dt = gaussian(arg_keys[5], (LAYERS, D, HM), D ** -0.5, 0.1875, ((2, 4),))
    w_bc = gaussian(arg_keys[6], (LAYERS, D, 2 * NS), D ** -0.5, 0.1875)
    conv_x = gaussian(arg_keys[7], (LAYERS, HM * HP, 4), 4 ** -0.5, 3.0, ((1, 4),))
    conv_bc = gaussian(arg_keys[8], (LAYERS, 2 * NS, 4), 4 ** -0.5, 3.0)
    dt_bias = jnp.clip(-4.0 + 2.0 * jax.random.uniform(arg_keys[9], (LAYERS, HM), jnp.float32) ** steps_of(arg_keys[9], (LAYERS, HM), ((1, 4),), -0.2, 0.2), -4.0, -2.0)
    a_log = jnp.clip(-3.0 + 3.5 * jax.random.uniform(arg_keys[10], (LAYERS, HM), jnp.float32) ** steps_of(arg_keys[10], (LAYERS, HM), ((1, 4),), -0.2, 0.2), -3.0, 0.5)
    d_skip = jnp.clip(0.5 + 1.0 * jax.random.uniform(arg_keys[11], (LAYERS, HM), jnp.float32) ** steps_of(arg_keys[11], (LAYERS, HM), ((1, 4),), -0.2, 0.2), 0.5, 1.5)
    w_q = gaussian(arg_keys[12], (LAYERS, D, HQ * HD), D ** -0.5, 0.1875, ((2, 4),))
    w_kv = gaussian(arg_keys[13], (LAYERS, D, 2, HK * HD), D ** -0.5, 0.1875)
    w_o = gaussian(arg_keys[14], (LAYERS, D, HQ * HD), (HQ * HD // 16) ** -0.5, 1.0, ((2, 4),))
    w_out = gaussian(arg_keys[15], (LAYERS, D, HM * HP), (HM * HP) ** -0.5, 0.15625, ((2, 4),))
    norm_ffn = jnp.clip(1.0 + 0.1 * jax.random.normal(arg_keys[16], (LAYERS, D), jnp.float32), 0.5, 1.5).astype(jnp.bfloat16)
    w_gu = gaussian(arg_keys[17], (LAYERS, D, 2, FF), D ** -0.5, 0.1875, ((3, 4),))
    w_down = gaussian(arg_keys[18], (LAYERS, D, FF), FF ** -0.5, 0.125, ((2, 4),))
    return dict(hidden_in=hidden_in, segments=segments, cotangent=cotangent, norm_attn=norm_attn, w_zx=w_zx, w_dt=w_dt, w_bc=w_bc, conv_x=conv_x, conv_bc=conv_bc, dt_bias=dt_bias, a_log=a_log, d_skip=d_skip, w_q=w_q, w_kv=w_kv, w_o=w_o, w_out=w_out, norm_ffn=norm_ffn, w_gu=w_gu, w_down=w_down)


EPSILON = 1e-05
HIGHEST = lax.Precision.HIGHEST
MASKED = -1e+30

@jax.custom_vjp
def low(v):
    return lax.optimization_barrier(v.astype(jnp.bfloat16)).astype(jnp.float32)

@jax.custom_vjp
def low_back(v):
    return v

def low_keep(v):
    return (low(v), None)

def low_pass(kept, grad):
    return (grad,)

def back_keep(v):
    return (v, None)

def back_low(kept, grad):
    return (low(grad),)
low.defvjp(low_keep, low_pass)
low_back.defvjp(back_keep, back_low)

def rms_norm(values, gain_vec):
    return values * lax.rsqrt(lax.optimization_barrier(jnp.mean(values * values, axis=-1, keepdims=True)) + EPSILON) * gain_vec

def rotary(values, positions):
    half_size = HD // 2
    freq_steps = jnp.arange(half_size).astype(jnp.float32) * (2.0 / HD)
    frequency = jnp.exp(-jnp.log(10000.0) * freq_steps)
    angles = positions.astype(jnp.float32)[:, None] * frequency[None, :]
    cosine = jnp.cos(angles)[:, None, :]
    sine_vals = jnp.sin(angles)[:, None, :]
    first_half = values[..., :half_size]
    second_half = values[..., half_size:]
    return jnp.concatenate([first_half * cosine - second_half * sine_vals, second_half * cosine + first_half * sine_vals], axis=-1)

def short_conv(conv_in, kernel, seg_row):
    length = conv_in.shape[0]
    padded = jnp.concatenate([jnp.zeros((3, conv_in.shape[1]), conv_in.dtype), conv_in], axis=0)
    seg_pad = jnp.concatenate([jnp.full((3,), -1, jnp.int32), seg_row])
    total_sum = jnp.zeros_like(conv_in)
    for tap_index in range(4):
        tap_keep = (seg_pad[tap_index:tap_index + length] == seg_row).astype(conv_in.dtype)
        total_sum = total_sum + padded[tap_index:tap_index + length] * kernel[:, tap_index][None, :] * tap_keep[:, None]
    return total_sum

def state_space(inner_vals, b_mat, c_mat, step_size, log_decay, seg_row):
    length = inner_vals.shape[0]
    cumulative = jnp.cumsum(log_decay, axis=0)
    order_ok = jnp.arange(length)[:, None] >= jnp.arange(length)[None, :]
    same_doc = ((seg_row[:, None] == seg_row[None, :]) & order_ok)[None]
    log_gaps = cumulative.T[:, :, None] - cumulative.T[:, None, :]
    decay_mat = jnp.where(same_doc, jnp.exp(jnp.where(same_doc, log_gaps, 0.0)), 0.0)
    scores = jnp.dot(c_mat, b_mat.T, precision=HIGHEST)
    mixing = scores[None] * decay_mat * step_size.T[:, None, :]
    return jnp.einsum('hts,shp->thp', mixing, inner_vals, precision=HIGHEST)

def mamba_branch(normed, seg_row, weights_one):
    w_zx, w_dt, w_bc, conv_x, conv_bc, dt_bias, a_log, d_skip, w_out = weights_one
    length = normed.shape[0]
    zx_both = jnp.einsum('td,dgk->tgk', normed, w_zx, precision=HIGHEST)
    gate_in = low_back(zx_both[:, 0])
    inner_in = low(low_back(zx_both[:, 1]))
    step_raw = low_back(jnp.dot(normed, w_dt, precision=HIGHEST))
    state_in = low(jnp.dot(normed, w_bc, precision=HIGHEST))
    conv_in = jnp.concatenate([inner_in, state_in], axis=1)
    kernel = jnp.concatenate([conv_x, conv_bc], axis=0)
    activated = jax.nn.silu(short_conv(conv_in, kernel, seg_row))
    inner_dim = HM * HP
    inner_vals = activated[:, :inner_dim].reshape(length, HM, HP)
    b_mat = activated[:, inner_dim:inner_dim + NS]
    c_mat = activated[:, inner_dim + NS:]
    step_size = jax.nn.softplus(step_raw + dt_bias)
    log_decay = -jnp.exp(a_log) * step_size
    ssm_out = state_space(inner_vals, b_mat, c_mat, step_size, log_decay, seg_row) + d_skip[None, :, None] * inner_vals
    gated_out = low(ssm_out.reshape(length, inner_dim) * jax.nn.silu(gate_in))
    return jnp.dot(gated_out, w_out.T, precision=HIGHEST)

def attention_branch(normed, seg_row, positions, weights_one):
    w_q, w_kv, w_o = weights_one
    length = normed.shape[0]
    query_pre = low_back(jnp.dot(normed, w_q, precision=HIGHEST)).reshape(length, HQ, HD)
    queries = low(rotary(query_pre, positions))
    key_vals = jnp.einsum('td,dgk->tgk', normed, w_kv, precision=HIGHEST)
    key_heads = low(rotary(key_vals[:, 0].reshape(length, HK, HD), positions))
    value_heads = low(key_vals[:, 1].reshape(length, HK, HD))
    key_heads = jnp.repeat(key_heads, HQ // HK, axis=1)
    value_heads = jnp.repeat(value_heads, HQ // HK, axis=1)
    scores = low_back(jnp.einsum('thd,shd->hts', queries, key_heads, precision=HIGHEST) * HD ** (-0.5))
    allowed = (seg_row[:, None] == seg_row[None, :]) & (positions[:, None] >= positions[None, :])
    scores = jnp.where(allowed[None], scores, MASKED)
    top_score = lax.optimization_barrier(jnp.max(scores, axis=-1, keepdims=True))
    weights = jnp.exp(scores - top_score)
    prob_mat = low(weights / lax.optimization_barrier(jnp.sum(weights, axis=-1, keepdims=True)))
    attended = jnp.einsum('hts,shd->thd', prob_mat, value_heads, precision=HIGHEST)
    attended = low(low_back(attended)).reshape(length, HQ * HD)
    return jnp.dot(attended, w_o.T, precision=HIGHEST)

def hybrid_block(residual, seg_row, positions, weights_one):
    norm_attn, w_zx, w_dt, w_bc, conv_x, conv_bc, dt_bias, a_log, d_skip, w_q, w_kv, w_o, w_out, norm_ffn, w_gu, w_down = weights_one
    normed = low(rms_norm(residual, norm_attn))
    mixer_out = attention_branch(normed, seg_row, positions, (w_q, w_kv, w_o))
    mixer_out = mixer_out + mamba_branch(normed, seg_row, (w_zx, w_dt, w_bc, conv_x, conv_bc, dt_bias, a_log, d_skip, w_out))
    hidden = residual + low_back(mixer_out)
    normed_ffn = low(rms_norm(hidden, norm_ffn))
    gate_up = low_back(jnp.einsum('td,dgf->tgf', normed_ffn, w_gu, precision=HIGHEST))
    swiglu = low(jax.nn.silu(gate_up[:, 0]) * gate_up[:, 1])
    return hidden + low_back(jnp.dot(swiglu, w_down.T, precision=HIGHEST))

def reference(hidden_in, segments, cotangent, norm_attn, w_zx, w_dt, w_bc, conv_x, conv_bc, dt_bias, a_log, d_skip, w_q, w_kv, w_o, w_out, norm_ffn, w_gu, w_down):
    params = tuple((member.astype(jnp.float32) for member in (norm_attn, w_zx, w_dt, w_bc, conv_x, conv_bc, dt_bias, a_log, d_skip, w_q, w_kv, w_o, w_out, norm_ffn, w_gu, w_down)))
    positions = jnp.arange(LEN).astype(jnp.int32)

    def one_sequence(totals, inputs):
        resid_row, seg_row, cot_row = inputs

        def forward(weights_all, residual):
            for layer_id in range(LAYERS):
                residual = hybrid_block(residual, seg_row, positions, tuple((member[layer_id] for member in weights_all)))
            return residual
        result, pullback = jax.vjp(forward, params, resid_row)
        grad_params, grad_resid = pullback(cot_row)
        totals = tuple((running + grad_term for running, grad_term in zip(totals, grad_params)))
        return (totals, (result, grad_resid))
    zero_grads = tuple((jnp.zeros_like(member) for member in params))
    totals, (outputs, grad_rows) = lax.scan(one_sequence, zero_grads, (hidden_in.astype(jnp.float32), segments, cotangent.astype(jnp.float32)))
    return (outputs.astype(jnp.bfloat16), grad_rows, totals[0], totals[1], totals[2], totals[3], totals[4], totals[5], totals[6], totals[7], totals[8], totals[9], totals[10], totals[11], totals[12], totals[13], totals[14], totals[15])
```

```python
import jax
import jax.numpy as jnp
from jax import lax
from jax.experimental import pallas as pl
from jax.experimental.pallas import tpu as pltpu
from jax.sharding import PartitionSpec as P

HP = 64
NS = 128
HQ = 8
HK = 2
HD = 64
EPSILON = 1e-05
HIGHEST = lax.Precision.HIGHEST
MASKED = -1e30
F32 = jnp.float32
BF16 = jnp.bfloat16

GATE, QUERY, INNER, STATE, KEYVAL, STEP = 0, 384, 512, 896, 1152, 1280
WIDTH = 1408
EARLY = 512
CONV = 640
ROWS = 256


def shifted(x, axis, distance):
    count = lax.axis_size(axis)
    route = [(i, i + distance) for i in range(count) if 0 <= i + distance < count]
    return lax.ppermute(x, axis, route)


def swapped(x, distance):
    return lax.ppermute(x, "tensor", [(i, i ^ distance) for i in range(4)])


def reduce_half(part):
    core = lax.axis_index("tensor") & 1
    both = part.reshape(2, part.shape[0] // 2, part.shape[1])
    mine = lax.dynamic_index_in_dim(both, core, 0, keepdims=False)
    other = lax.dynamic_index_in_dim(both, 1 - core, 0, keepdims=False)
    chip = (mine.astype(F32) + swapped(other, 1).astype(F32)).astype(BF16)
    return chip.astype(F32) + swapped(chip, 2).astype(F32)


def own_half(x):
    core = lax.axis_index("tensor") & 1
    return lax.dynamic_slice_in_dim(x, core * (x.shape[0] // 2), x.shape[0] // 2, 0)


def both_halves(x):
    core = (lax.axis_index("tensor") & 1).astype(jnp.int32).reshape(1)
    return core, x, swapped(x, 1)


def gather_half(x):
    core = lax.axis_index("tensor") & 1
    other = swapped(x, 1)
    first = jnp.where(core == 0, x, other)
    second = jnp.where(core == 0, other, x)
    return jnp.concatenate([first, second], axis=0)


def mm(a, b):
    return lax.dot_general(a, b, (((1,), (0,)), ((), ())), preferred_element_type=F32)


def mm_t(a, b):
    return lax.dot_general(a, b, (((1,), (1,)), ((), ())), preferred_element_type=F32)


def t_mm(a, b):
    return lax.dot_general(a, b, (((0,), (0,)), ((), ())), preferred_element_type=F32)


def iota(shape, dim):
    return lax.broadcasted_iota(jnp.int32, shape, dim)


def softplus(x):
    return jnp.maximum(x, 0.0) + jnp.log1p(jnp.exp(-jnp.abs(x)))


def sigmoid(x):
    return 1.0 / (1.0 + jnp.exp(-x))


def pair_lanes(columns, j, rows):
    low = iota((rows, 128), 1) < 64
    return jnp.where(low, columns[:, 2 * j : 2 * j + 1], columns[:, 2 * j + 1 : 2 * j + 2])


def pair_sums(values, j, rows):
    low = iota((rows, 128), 1) < 64
    first = jnp.sum(jnp.where(low, values, 0.0), axis=1, keepdims=True)
    second = jnp.sum(jnp.where(low, 0.0, values), axis=1, keepdims=True)
    lane = iota((rows, 128), 1)
    return jnp.where(lane == 2 * j, first, 0.0) + jnp.where(lane == 2 * j + 1, second, 0.0)


def place_halves(core, own, other, full):
    half = ROWS // 2
    full[pl.ds(pl.multiple_of(core[0] * half, half), half), :] = own[...]
    full[pl.ds(pl.multiple_of((1 - core[0]) * half, half), half), :] = other[...]


def turn(x, cosine, sine):
    lane = iota(x.shape, 1) % 64
    ahead = pltpu.roll(x, 96, 1)
    behind = pltpu.roll(x, 32, 1)
    return x * cosine + jnp.where(lane < 32, -ahead, behind) * sine


def call(kernel, outs, args, scratch=(), flops=10**8):
    size = sum(a.size * a.dtype.itemsize for a in args)
    return pl.pallas_call(
        kernel,
        out_shape=[jax.ShapeDtypeStruct(s, d) for s, d in outs],
        in_specs=[
            pl.BlockSpec(memory_space=pltpu.SMEM if a.dtype == jnp.int32 else pltpu.VMEM)
            for a in args
        ],
        out_specs=[pl.BlockSpec(memory_space=pltpu.VMEM) for _ in outs],
        scratch_shapes=list(scratch),
        compiler_params=pltpu.CompilerParams(vmem_limit_bytes=40 * 1024 * 1024),
        cost_estimate=pl.CostEstimate(flops=flops, bytes_accessed=size, transcendentals=0),
    )(*args)


def project_kernel(core, own, other, w_all, cos, sin, normed_o, proj_o, q_o, sent_o):
    place_halves(core, own, other, normed_o)
    normed = normed_o[...]
    for at in ((KEYVAL, WIDTH), (QUERY, INNER), (INNER, KEYVAL), (GATE, QUERY)):
        proj_o[:, at[0] : at[1]] = mm(normed, w_all[:, at[0] : at[1]])
    q_o[...] = turn(proj_o[:, QUERY:INNER], cos[...], sin[...]).astype(BF16)
    is_key = iota((ROWS, 128), 1) < 64
    kv = proj_o[:, KEYVAL:STEP]
    sent_o[0:ROWS, :] = jnp.where(is_key, turn(kv, cos[...], sin[...]), kv).astype(BF16)
    for j in range(5):
        sent_o[ROWS + 16 * j : ROWS + 16 * j + 16, :] = proj_o[
            ROWS - 16 : ROWS, INNER + 128 * j : INNER + 128 * j + 128
        ].astype(BF16)


def fill_extended(proj, near, ext):
    for j in range(5):
        at = slice(128 * j, 128 * j + 128)
        ext[0:8, at] = near[ROWS + 16 * j : ROWS + 16 * j + 16, :].astype(F32)[8:16, :]
    ext[8 : 8 + ROWS, :] = proj[:, INNER:KEYVAL].astype(BF16).astype(F32)


def feed_forward_kernel(core, own, other, w_gu, w_down, normed_o, gate_up_o, swiglu_o, out_o):
    place_halves(core, own, other, normed_o)
    gate_up_o[...] = mm(normed_o[...], w_gu[...])
    units = swiglu_o.shape[1]
    gate = gate_up_o[:, 0:units]
    swiglu_o[...] = (gate * sigmoid(gate) * gate_up_o[:, units : 2 * units]).astype(BF16)
    out_o[...] = mm_t(swiglu_o[...], w_down[...]).astype(BF16)


def ssm_local_kernel(proj, near, kern, heads, colp, segr, pre_o, yloc_o, stepcum_o, msg_o, ext):
    fill_extended(proj, near, ext)
    pre = jnp.zeros((ROWS, CONV), F32)
    for k in range(4):
        pre = pre + ext[5 + k : 5 + k + ROWS, :] * kern[k : k + 1, :] * colp[:, 2 + k : 3 + k]
    pre_o[...] = pre
    act = pre * sigmoid(pre)
    step = softplus(proj[:, STEP:WIDTH] + heads[0:1, :])
    decay = -jnp.exp(heads[1:2, :]) * step
    order = iota((ROWS, ROWS), 0) >= iota((ROWS, ROWS), 1)
    cum = jnp.dot(order.astype(F32), decay, precision=HIGHEST, preferred_element_type=F32)
    stepcum_o[:, 0:128] = step
    stepcum_o[:, 128:256] = cum
    cum_t = cum.T
    same = (colp[:, 0:1] == segr[0:1, 0:ROWS]) & order
    b_low = act[:, 384:512].astype(BF16)
    c_low = act[:, 512:640].astype(BF16)
    scores = mm_t(c_low, b_low)
    last = cum[ROWS - 1 : ROWS, :]
    tail = jnp.where(colp[:, 6:7] > 0.5, jnp.exp(last - cum), 0.0) * step
    low = iota((ROWS, 128), 1) < 64
    for j in range(3):
        tile = act[:, 128 * j : 128 * j + 128]
        scaled = (tile * pair_lanes(step, j, ROWS)).astype(BF16)
        sides = []
        for h in (2 * j, 2 * j + 1):
            gap = jnp.where(same, cum[:, h : h + 1] - cum_t[h : h + 1, :], MASKED)
            sides.append(mm((scores * jnp.exp(gap)).astype(BF16), scaled))
        yloc_o[:, 128 * j : 128 * j + 128] = jnp.where(low, sides[0], sides[1])
        weighted = (tile * pair_lanes(tail, j, ROWS)).astype(BF16)
        msg_o[128 * j : 128 * j + 128, :] = t_mm(weighted, b_low).astype(BF16)
    msg_o[384:400, :] = jnp.broadcast_to(
        jnp.exp(last) * colp[ROWS - 1 : ROWS, 1:2], (16, 128)
    ).astype(BF16)


def chained(m1, m2, m3, out):
    d1 = m1[384:392, :].astype(F32)
    d2 = m2[384:392, :].astype(F32)
    for h in range(6):
        at = slice(64 * h, 64 * h + 64)
        inner = m2[at, :].astype(F32) + d2[0:1, h : h + 1] * m3[at, :].astype(F32)
        out[at, :] = m1[at, :].astype(F32) + d1[0:1, h : h + 1] * inner


def mixer_kernel(
    proj, pre, yloc, stepcum, m1, m2, m3, heads, colp, att, w_o, w_out,
    state_o, y_o, feat_o, mixer_o,
):
    chained(m1, m2, m3, state_o)
    c_pre = pre[:, 512:640]
    c_low = (c_pre * sigmoid(c_pre)).astype(BF16)
    grow = jnp.exp(stepcum[:, 128:256]) * colp[:, 1:2]
    inflow = mm_t(c_low, state_o[...].astype(BF16))
    feat_o[:, 0:128] = att[...]
    for j in range(3):
        at = slice(128 * j, 128 * j + 128)
        y = yloc[:, at] + inflow[:, at] * pair_lanes(grow, j, ROWS)
        y_o[:, at] = y
        x_pre = pre[:, at]
        gate = proj[:, at]
        full = y + x_pre * sigmoid(x_pre) * pair_lanes(heads[2:3, :], j, 1)
        feat_o[:, 128 + 128 * j : 256 + 128 * j] = (full * gate * sigmoid(gate)).astype(BF16)
    mixer_o[...] = (
        mm_t(feat_o[:, 0:128], w_o[...]) + mm_t(feat_o[:, 128:512], w_out[...])
    ).astype(BF16)


def head_sides(q):
    low = iota(q.shape, 1) < 64
    return (
        jnp.where(low, q, 0.0),
        jnp.where(low, pltpu.roll(q, 64, 1), 0.0),
    )


def attention_kernel(q, kv0, kv1, kv2, kv3, colp, segr, att_o):
    kvs = [r[0:ROWS, :] for r in (kv0, kv1, kv2, kv3)]
    low = iota((ROWS, 128), 1) < 64
    seg_q = colp[:, 0:1]
    order = iota((ROWS, ROWS), 0) >= iota((ROWS, ROWS), 1)
    masks = [seg_q == segr[0:1, ROWS * k : ROWS * k + ROWS] for k in range(4)]
    masks[0] = masks[0] & order
    outs = []
    for side in head_sides(q[...].astype(F32)):
        side = (side * 0.125).astype(BF16)
        scores = [
            jnp.where(masks[k], mm_t(side, kvs[k]), MASKED)
            for k in range(4)
        ]
        top = jnp.max(scores[0], axis=1, keepdims=True)
        for k in range(1, 4):
            top = jnp.maximum(top, jnp.max(scores[k], axis=1, keepdims=True))
        weights = [jnp.exp(s - top) for s in scores]
        total = sum(jnp.sum(w, axis=1, keepdims=True) for w in weights)
        inv = 1.0 / total
        out = jnp.zeros((ROWS, 128), F32)
        for k in range(4):
            out = out + mm((weights[k] * inv).astype(BF16), kvs[k])
        outs.append(out)
    att_o[...] = jnp.where(low, pltpu.roll(outs[0], 64, 1), outs[1]).astype(BF16)


def attention_back_kernel(
    q, kv0, kv1, kv2, kv3, colp, segr, datt, cos, sin, dq_o, own_o, sent_o
):
    kvs = [r[0:ROWS, :] for r in (kv0, kv1, kv2, kv3)]
    low = iota((ROWS, 128), 1) < 64
    seg_q = colp[:, 0:1]
    order = iota((ROWS, ROWS), 0) >= iota((ROWS, ROWS), 1)
    masks = [seg_q == segr[0:1, ROWS * k : ROWS * k + ROWS] for k in range(4)]
    masks[0] = masks[0] & order
    d_out = datt[...].astype(F32)
    d_sides = (
        jnp.where(low, 0.0, pltpu.roll(d_out, 64, 1)).astype(BF16),
        jnp.where(low, 0.0, d_out).astype(BF16),
    )
    grads = [jnp.zeros((ROWS, 128), F32) for _ in range(4)]
    dqs = []
    for side, d_side in zip(head_sides(q[...].astype(F32)), d_sides):
        side = (side * 0.125).astype(BF16)
        scores = [
            jnp.where(masks[k], mm_t(side, kvs[k]), MASKED)
            for k in range(4)
        ]
        top = jnp.max(scores[0], axis=1, keepdims=True)
        for k in range(1, 4):
            top = jnp.maximum(top, jnp.max(scores[k], axis=1, keepdims=True))
        weights = [jnp.exp(s - top) for s in scores]
        total = sum(jnp.sum(w, axis=1, keepdims=True) for w in weights)
        inv = 1.0 / total
        probs = [w * inv for w in weights]
        d_probs = [mm_t(d_side, kvs[k]) for k in range(4)]
        inner = sum(jnp.sum(p * d, axis=1, keepdims=True) for p, d in zip(probs, d_probs))
        dq = jnp.zeros((ROWS, 128), F32)
        for k in range(4):
            d_scores = (probs[k] * (d_probs[k] - inner)).astype(BF16)
            dq = dq + mm(d_scores, kvs[k])
            grads[k] = grads[k] + t_mm(d_scores, side) + t_mm(probs[k].astype(BF16), d_side)
        dqs.append(dq * 0.125)
    dq = jnp.where(low, dqs[0], pltpu.roll(dqs[1], 64, 1))
    dq_o[...] = turn(dq, cos[...], -sin[...]).astype(BF16)
    own_o[...] = grads[0]
    for k in range(1, 4):
        sent_o[k - 1] = grads[k].astype(BF16)


def finish_back_kernel(
    core, own, other, w_o, w_out, proj, pre, y, stepcum, state, heads, colp,
    gm, datt_o, dgate_o, dy_o, dc_o, msg_o, grown,
):
    place_halves(core, own, other, gm)
    datt_o[...] = mm(gm[...], w_o[...]).astype(BF16)
    d_gated = mm(gm[...], w_out[...])
    grow = jnp.exp(stepcum[:, 128:256]) * colp[:, 1:2]
    for j in range(3):
        at = slice(128 * j, 128 * j + 128)
        x_pre = pre[:, at]
        full = y[:, at] + x_pre * sigmoid(x_pre) * pair_lanes(heads[2:3, :], j, 1)
        gate = proj[:, at]
        sig = sigmoid(gate)
        dy = (d_gated[:, at] * gate * sig).astype(BF16)
        dgate_o[:, at] = (d_gated[:, at] * full * sig * (1.0 + gate * (1.0 - sig))).astype(BF16)
        dy_o[:, at] = dy
        grown[:, at] = (dy.astype(F32) * pair_lanes(grow, j, ROWS)).astype(BF16)
    c_pre = pre[:, 512:640]
    c_low = (c_pre * sigmoid(c_pre)).astype(BF16)
    dc_o[...] = mm(grown[...], state[...].astype(BF16))
    msg_o[0:384, :] = t_mm(grown[...], c_low).astype(BF16)
    msg_o[384:400, :] = jnp.broadcast_to(grow[ROWS - 1 : ROWS, :], (16, 128)).astype(BF16)


def ssm_back_kernel(pre, stepcum, dy, dc, colp, segr, dxs_o, db_o, dc_o):
    step = stepcum[:, 0:128]
    cum = stepcum[:, 128:256]
    cum_t = cum.T
    order = iota((ROWS, ROWS), 0) >= iota((ROWS, ROWS), 1)
    same = (colp[:, 0:1] == segr[0:1, 0:ROWS]) & order
    bc = pre[:, 384:640]
    bc = (bc * sigmoid(bc)).astype(BF16)
    b_low, c_low = bc[:, 0:128], bc[:, 128:256]
    scores = mm_t(c_low, b_low)
    d_scores = jnp.zeros((ROWS, ROWS), F32)
    low = iota((ROWS, 128), 1) < 64
    for j in range(3):
        at = slice(128 * j, 128 * j + 128)
        x_pre = pre[:, at]
        scaled = (x_pre * sigmoid(x_pre) * pair_lanes(step, j, ROWS)).astype(BF16)
        dy_low = dy[:, at]
        zero = jnp.zeros_like(dy_low)
        sides = []
        for h in (2 * j, 2 * j + 1):
            decay = jnp.exp(jnp.where(same, cum[:, h : h + 1] - cum_t[h : h + 1, :], MASKED))
            own = jnp.where(low if h == 2 * j else ~low, dy_low, zero)
            d_scores = d_scores + mm_t(own, scaled) * decay
            sides.append(t_mm((scores * decay).astype(BF16), dy_low))
        dxs_o[:, at] = jnp.where(low, sides[0], sides[1])
    d_low = d_scores.astype(BF16)
    db_o[...] = t_mm(d_low, c_low)
    dc_o[...] = dc[...] + mm(d_low, b_low)


def conv_back_kernel(
    proj, near, kern, heads, colp, pre, stepcum, dy, y, dxs, db, dc, state, n1, n2, n3,
    dconv_o, rim_o, dstep_o, small_o, carry, weighted, dact, ext, dext,
):
    chained(n1, n2, n3, carry)
    step = stepcum[:, 0:128]
    cum = stepcum[:, 128:256]
    b_pre = pre[:, 384:512]
    b_low = (b_pre * sigmoid(b_pre)).astype(BF16)
    carry_low = carry[...].astype(BF16)
    spread = mm_t(b_low, carry_low)
    last = cum[ROWS - 1 : ROWS, :]
    tail = jnp.where(colp[:, 6:7] > 0.5, jnp.exp(last - cum), 0.0)
    d_cum = jnp.zeros((ROWS, 128), F32)
    d_step = jnp.zeros((ROWS, 128), F32)
    d_tail = jnp.zeros((ROWS, 128), F32)
    d_skip = jnp.zeros((1, 128), F32)
    for j in range(3):
        at = slice(128 * j, 128 * j + 128)
        x_pre = pre[:, at]
        x = x_pre * sigmoid(x_pre)
        dy_at = dy[:, at].astype(F32)
        step_at = pair_lanes(step, j, ROWS)
        d_scaled = dxs[:, at] + spread[:, at] * pair_lanes(tail, j, ROWS)
        dact[:, at] = d_scaled * step_at + dy_at * pair_lanes(heads[2:3, :], j, 1)
        d_step = d_step + pair_sums(d_scaled * x, j, ROWS)
        weighted[:, at] = (x * pair_lanes(tail * step, j, ROWS)).astype(BF16)
        d_tail = d_tail + pair_sums(weighted[:, at].astype(F32) * spread[:, at], j, ROWS)
        scaled = (x * step_at).astype(BF16).astype(F32)
        d_cum = d_cum + pair_sums(dy_at * y[:, at] - scaled * dxs[:, at], j, ROWS)
        d_skip = d_skip + pair_sums(jnp.sum(dy_at * x, axis=0, keepdims=True), j, 1)
    dact[:, 384:512] = db[...] + mm(weighted[...], carry_low)
    dact[:, 512:640] = dc[...]
    d_cum = d_cum - d_tail
    d_decay = jnp.zeros((1, 128), F32)
    lane = iota((1, 128), 1)
    for h in range(6):
        hs = slice(64 * h, 64 * h + 64)
        d_decay = d_decay + jnp.where(lane == h, jnp.sum(carry[hs, :] * state[hs, :]), 0.0)
    d_last = (
        jnp.sum(d_tail, axis=0, keepdims=True)
        + d_decay * jnp.exp(last) * colp[ROWS - 1 : ROWS, 1:2]
    )
    later = iota((ROWS, ROWS), 0) <= iota((ROWS, ROWS), 1)
    d_log = d_last + jnp.dot(
        later.astype(F32), d_cum, precision=HIGHEST, preferred_element_type=F32
    )
    rate = -jnp.exp(heads[1:2, :])
    d_step = d_step + rate * d_log
    raw = proj[:, STEP:WIDTH] + heads[0:1, :]
    real = iota((ROWS, 128), 1) < 6
    d_raw = jnp.where(real, d_step * sigmoid(raw), 0.0)
    dstep_o[...] = d_raw.astype(BF16)
    small_o[...] = jnp.zeros((8, CONV), F32)
    small_o[4:5, 0:128] = jnp.sum(d_raw, axis=0, keepdims=True)
    small_o[5:6, 0:128] = jnp.sum(d_log * rate * step, axis=0, keepdims=True)
    small_o[6:7, 0:128] = d_skip
    fill_extended(proj, near, ext)
    sig = sigmoid(pre[...])
    d_pre = dact[...] * sig * (1.0 + pre[...] * (1.0 - sig))
    dext[...] = jnp.zeros((8 + ROWS, CONV), F32)
    for k in range(4):
        kept = d_pre * colp[:, 2 + k : 3 + k]
        rows = slice(5 + k, 5 + k + ROWS)
        small_o[k : k + 1, :] = jnp.sum(ext[rows, :] * kept, axis=0, keepdims=True)
        dext[rows, :] = dext[rows, :] + kept * kern[k : k + 1, :]
    rim_o[...] = dext[0:8, :]
    dconv_o[...] = dext[8 : 8 + ROWS, :]


def feed_forward_back_kernel(
    core, own, other, gate_up, w_gu, w_down, normed, gain, grad_o, d_gu_o, part_o, prod_o
):
    place_halves(core, own, other, grad_o)
    d_swiglu = mm(grad_o[...], w_down[...])
    units = d_swiglu.shape[1]
    gate = gate_up[:, 0:units]
    up = gate_up[:, units : 2 * units]
    sig = sigmoid(gate)
    d_gu_o[:, 0:units] = (d_swiglu * up * sig * (1.0 + gate * (1.0 - sig))).astype(BF16)
    d_gu_o[:, units : 2 * units] = (d_swiglu * gate * sig).astype(BF16)
    part = mm_t(d_gu_o[...], w_gu[...])
    part_o[...] = part.astype(BF16)
    prod_o[...] = (part * normed[...].astype(F32) / gain[...]).astype(BF16)


def feed_forward_weights_kernel(grad, swiglu, normed, d_gu, out_o):
    wide = d_gu.shape[1]
    out_o[:, 0:wide] = t_mm(normed[...], d_gu[...]).astype(BF16)
    out_o[:, wide:] = t_mm(grad[...], swiglu[...]).astype(BF16)


def mixer_weights_kernel(normed, dgate, dq, gm, feat, out_o):
    out_o[:, 0:384] = t_mm(normed[...], dgate[...]).astype(BF16)
    out_o[:, 384:512] = t_mm(normed[...], dq[...]).astype(BF16)
    out_o[:, 512:1024] = t_mm(gm[...], feat[...]).astype(BF16)


def normed_back_kernel(
    dgate, dq, dconv, rim, dkv, k1, k2, k3, dstep, w_all, normed, gain, cos, sin,
    late_o, part_o, prod_o,
):
    late_o[0 : ROWS - 16, 0:CONV] = dconv[0 : ROWS - 16, :].astype(BF16)
    end = dconv[ROWS - 16 : ROWS, :]
    end = end + jnp.concatenate([jnp.zeros((8, CONV), F32), rim[...]], axis=0)
    late_o[ROWS - 16 : ROWS, 0:CONV] = end.astype(BF16)
    kv = dkv[...] + k1[...].astype(F32) + k2[...].astype(F32) + k3[...].astype(F32)
    is_key = iota((ROWS, 128), 1) < 64
    kv = jnp.where(is_key, turn(kv, cos[...], -sin[...]), kv)
    late_o[:, CONV : CONV + 128] = kv.astype(BF16)
    late_o[:, CONV + 128 : CONV + 256] = dstep[...]
    part = (
        mm_t(dgate[...], w_all[:, GATE:QUERY])
        + mm_t(dq[...], w_all[:, QUERY:INNER])
        + mm_t(late_o[...], w_all[:, INNER:WIDTH])
    )
    part_o[...] = part.astype(BF16)
    prod_o[...] = (part * normed[...].astype(F32) / gain[...]).astype(BF16)


def late_weights_kernel(normed, late, prod_attn, prod_ffn, extra, out_o):
    wide = CONV + 128
    out_o[:, 0:wide] = t_mm(normed[...], late[:, 0:wide]).astype(BF16)
    ones = jnp.ones((ROWS, 128), BF16)
    lane = iota((out_o.shape[0], 128), 1)
    block = jnp.where(lane < 6, t_mm(normed[...], late[:, wide:]), extra[...])
    block = jnp.where(lane == 6, t_mm(prod_attn[...], ones), block)
    block = jnp.where(lane == 7, t_mm(prod_ffn[...], ones), block)
    out_o[:, wide:] = block.astype(BF16)


def rms_scale(x):
    return lax.rsqrt(jnp.mean(x * x, axis=-1, keepdims=True) + EPSILON)


def rms_back(grad, x, gain):
    scale = rms_scale(x)
    g = grad * gain
    return g * scale - x * (scale**3) * jnp.mean(g * x, axis=-1, keepdims=True)


def to_owner(grad):
    count = lax.axis_size("dp") * lax.axis_size("ctx")
    rows = grad.shape[0] // count
    got = lax.all_to_all(grad.reshape(count, rows, -1), ("dp", "ctx"), 0, 0, tiled=True)
    return jnp.sum(got.astype(F32), axis=0)


def extra_lanes(small):
    sums = small[4:7, :6].reshape(18)
    high = sums.astype(BF16)
    low = (sums - high.astype(F32)).astype(BF16)
    sums = jnp.pad(jnp.concatenate([high, low]).astype(F32), (0, 28)).reshape(2, 32).T
    taps = small[:4, :384].reshape(32, 48)
    same = jnp.concatenate([jnp.zeros((32, 9), F32), sums, jnp.zeros((32, 5), F32), taps], axis=1)
    same = jnp.tile(jnp.pad(same, ((0, 0), (0, 64))), (32, 1))
    state = small[:4, 384:].T.reshape(1024, 1)
    return same + jnp.pad(state, ((0, 0), (8, 119)))


def body(
    hidden_in, segments, cotangent, norm_attn, w_zx, w_dt, w_bc, conv_x, conv_bc, dt_bias,
    a_log, d_skip, w_q, w_kv, w_o, w_out, norm_ffn, w_gu, w_down,
):
    layers, width = norm_attn.shape
    rows = hidden_in.shape[1]
    ctx = lax.axis_index("ctx")
    tensor = lax.axis_index("tensor")
    seg_row = segments[0]
    start = ctx * rows
    seg_pad = jnp.concatenate([jnp.full((3 * rows,), -1, jnp.int32), seg_row])
    windows = [
        lax.dynamic_slice_in_dim(seg_pad, start + (3 - k) * rows, rows) for k in range(4)
    ]
    here = windows[0]
    segr = jnp.concatenate(windows).astype(F32)[None]
    near = lax.dynamic_slice_in_dim(seg_pad, start + 3 * rows - 3, rows + 3)
    columns = [here.astype(F32), (here == near[2]).astype(F32)]
    columns += [(near[k : k + rows] == here).astype(F32) for k in range(4)]
    columns += [(here == here[-1]).astype(F32)]
    colp = jnp.pad(jnp.stack(columns, axis=1), ((0, 0), (0, 121)))
    positions = (start + jnp.arange(rows)).astype(F32)
    lane = jnp.arange(128) % 32
    frequency = jnp.exp(-jnp.log(10000.0) * lane.astype(F32) * (2.0 / HD))
    angles = positions[:, None] * frequency[None]
    cos, sin = jnp.cos(angles), jnp.sin(angles)
    kv_head = tensor // 2
    units = w_down.shape[2]

    saved = []
    full = hidden_in[0].astype(F32)
    resid = own_half(full)
    for l in range(layers):
        kv_w = lax.dynamic_slice_in_dim(w_kv[l], kv_head * HD, HD, axis=2).reshape(width, 2 * HD)
        w_all = jnp.concatenate(
            [
                w_zx[l, :, 0], w_q[l], w_zx[l, :, 1], w_bc[l], kv_w,
                jnp.pad(w_dt[l], ((0, 0), (0, 122))),
            ],
            axis=1,
        )
        gate_up_w = w_gu[l].reshape(width, -1)
        kern = jnp.concatenate([conv_x[l], conv_bc[l]], axis=0).astype(F32).T
        heads = jnp.pad(
            jnp.stack([dt_bias[l], a_log[l], d_skip[l]]), ((0, 5), (0, 122))
        )
        gain_attn = norm_attn[l].astype(F32)[None]
        gain_ffn = norm_ffn[l].astype(F32)[None]
        if l == 0:
            normed = (full * rms_scale(full) * gain_attn).astype(BF16)
            core = (tensor & 1).astype(jnp.int32).reshape(1)
            halves = normed.reshape(2, rows // 2, width)
            parts = [lax.dynamic_index_in_dim(halves, i, 0, False) for i in (core[0], 1 - core[0])]
            halves = (core, *parts)
        else:
            halves = both_halves((resid * rms_scale(resid) * gain_attn).astype(BF16))
        normed, proj, q, sent = call(
            project_kernel,
            [((rows, width), BF16), ((rows, WIDTH), F32), ((rows, 128), BF16), ((336, 128), BF16)],
            (*halves, w_all, cos, sin),
        )
        kvs = (
            sent, shifted(sent, "ctx", 1),
            *(shifted(sent[:rows], "ctx", k) for k in (2, 3)),
        )
        pre, yloc, stepcum, msg = call(
            ssm_local_kernel,
            [((rows, CONV), F32), ((rows, 384), F32), ((rows, 256), F32), ((400, 128), BF16)],
            (proj, kvs[1], kern, heads, colp, segr),
            [pltpu.VMEM((8 + ROWS, CONV), F32)],
        )
        states = [shifted(msg, "ctx", k) for k in (1, 2, 3)]
        (att,) = call(attention_kernel, [((rows, 128), BF16)], (q, *kvs, colp, segr))
        state, y, feat, mixer = call(
            mixer_kernel,
            [((384, 128), F32), ((rows, 384), F32), ((rows, 512), BF16), ((rows, width), BF16)],
            (proj, pre, yloc, stepcum, *states, heads, colp, att, w_o[l], w_out[l]),
        )
        hidden = resid + reduce_half(mixer)
        halves = both_halves((hidden * rms_scale(hidden) * gain_ffn).astype(BF16))
        normed_ffn, gate_up, swiglu, ffn = call(
            feed_forward_kernel,
            [((rows, width), BF16), ((rows, 2 * units), F32), ((rows, units), BF16),
             ((rows, width), BF16)],
            (*halves, gate_up_w, w_down[l]),
        )
        saved.append(
            dict(
                w_all=w_all, gate_up_w=gate_up_w, kern=kern, heads=heads, gain_attn=gain_attn,
                gain_ffn=gain_ffn, resid=resid, normed=normed, proj=proj, q=q, kvs=kvs,
                pre=pre, stepcum=stepcum, state=state, y=y, feat=feat, hidden=hidden,
                normed_ffn=normed_ffn, gate_up=gate_up, swiglu=swiglu,
            )
        )
        resid = hidden + reduce_half(ffn)
    out = gather_half(resid.astype(BF16))

    grad = own_half(cotangent[0])
    owned = [None] * layers
    for l in reversed(range(layers)):
        s = saved[l]
        grad_ffn, d_gu, part, prod_ffn = call(
            feed_forward_back_kernel,
            [((rows, width), BF16), ((rows, 2 * units), BF16), ((rows, width), BF16),
             ((rows, width), BF16)],
            (*both_halves(grad.astype(BF16)), s["gate_up"], s["gate_up_w"], w_down[l],
             s["normed_ffn"], s["gain_ffn"]),
        )
        (weights_ffn,) = call(
            feed_forward_weights_kernel,
            [((width, 3 * units), BF16)],
            (grad_ffn, s["swiglu"], s["normed_ffn"], d_gu),
        )
        owned_ffn = to_owner(weights_ffn)
        total = reduce_half(part)
        grad_hidden = grad + rms_back(total, s["hidden"], s["gain_ffn"])
        gm, datt, dgate, dy, dc, msg = call(
            finish_back_kernel,
            [
                ((rows, width), BF16), ((rows, 128), BF16), ((rows, 384), BF16),
                ((rows, 384), BF16), ((rows, 128), F32), ((400, 128), BF16),
            ],
            (*both_halves(grad_hidden.astype(BF16)), w_o[l], w_out[l], s["proj"], s["pre"],
             s["y"], s["stepcum"], s["state"], s["heads"], colp),
            [pltpu.VMEM((ROWS, 384), BF16)],
        )
        carries = [shifted(msg, "ctx", -k) for k in (1, 2, 3)]
        dq, dkv_own, dkv_sent = call(
            attention_back_kernel,
            [((rows, 128), BF16), ((rows, 128), F32), ((3, rows, 128), BF16)],
            (s["q"], *s["kvs"], colp, segr, datt, cos, sin),
        )
        dkv_got = [shifted(dkv_sent[k - 1], "ctx", -k) for k in (1, 2, 3)]
        (weights_mid,) = call(
            mixer_weights_kernel,
            [((width, 1024), BF16)],
            (s["normed"], dgate, dq, gm, s["feat"]),
        )
        owned_mid = to_owner(weights_mid)
        dxs, db, dc = call(
            ssm_back_kernel,
            [((rows, 384), F32), ((rows, 128), F32), ((rows, 128), F32)],
            (s["pre"], s["stepcum"], dy, dc, colp, segr),
        )
        dconv, rim, dstep, small = call(
            conv_back_kernel,
            [((rows, CONV), F32), ((8, CONV), F32), ((rows, 128), BF16), ((8, CONV), F32)],
            (s["proj"], s["kvs"][1], s["kern"], s["heads"], colp, s["pre"], s["stepcum"], dy,
             s["y"], dxs, db, dc, s["state"], *carries),
            [
                pltpu.VMEM((384, 128), F32), pltpu.VMEM((ROWS, 384), BF16),
                pltpu.VMEM((ROWS, CONV), F32), pltpu.VMEM((8 + ROWS, CONV), F32),
                pltpu.VMEM((8 + ROWS, CONV), F32),
            ],
        )
        rim_got = shifted(rim, "ctx", -1)
        late, part, prod_attn = call(
            normed_back_kernel,
            [((rows, 896), BF16), ((rows, width), BF16), ((rows, width), BF16)],
            (dgate, dq, dconv, rim_got, dkv_own, *dkv_got, dstep, s["w_all"], s["normed"],
             s["gain_attn"], cos, sin),
        )
        (weights_late,) = call(
            late_weights_kernel,
            [((width, 896), BF16)],
            (s["normed"], late, prod_attn, prod_ffn, extra_lanes(small)),
        )
        owned_late = to_owner(weights_late)
        total = reduce_half(part)
        grad = grad_hidden + rms_back(total, s["resid"], s["gain_attn"])
        owned[l] = (owned_ffn, owned_mid, owned_late)
    grad_hidden_in = gather_half(grad)

    ffn, mid, late = (jnp.stack([owned[l][i] for l in range(layers)]) for i in range(3))
    shared = late[:, :, 384:].reshape(layers, 4, -1, 512)
    shared = lax.all_to_all(jnp.moveaxis(shared, 1, 0), "tensor", 0, 0, tiled=True)
    total = jnp.sum(shared, axis=0)
    head_kv = [jnp.sum(shared[2 * k : 2 * k + 2, ..., 256:384], axis=0) for k in range(2)]
    head_kv = [h.reshape(*h.shape[:-1], 2, HD) for h in head_kv]
    sums = (late[:, :, 777] + 0.0, late[:, :, 778])
    sums = jnp.concatenate(sums, axis=1)
    sums = (sums[:, :18] + sums[:, 18:36]).reshape(layers, 3, 6)
    taps = late[:, :, 784:832].reshape(layers, 4, 384)
    return (
        out[None],
        grad_hidden_in[None],
        total[..., 390],
        jnp.stack([mid[..., :384], late[..., :384]], axis=2),
        late[..., 768:774],
        total[..., :256],
        jnp.swapaxes(taps, 1, 2),
        total[..., 392].reshape(layers, 2, 4),
        sums[:, 0],
        sums[:, 1],
        sums[:, 2],
        mid[..., 384:512],
        jnp.concatenate(head_kv, axis=-1),
        mid[..., 512:640],
        mid[..., 640:1024],
        total[..., 391],
        ffn[..., : 2 * units].reshape(layers, -1, 2, units),
        ffn[..., 2 * units :],
    )


def solution(mesh):
    placed = (
        P("dp", "ctx", None),
        P("dp", None),
        P("dp", "ctx", None),
        P(),
        P(None, None, None, "tensor"),
        P(None, None, "tensor"),
        P(),
        P(None, "tensor", None),
        P(),
        P(None, "tensor"),
        P(None, "tensor"),
        P(None, "tensor"),
        P(None, None, "tensor"),
        P(),
        P(None, None, "tensor"),
        P(None, None, "tensor"),
        P(),
        P(None, None, None, "tensor"),
        P(None, None, "tensor"),
    )
    return jax.shard_map(
        body,
        mesh=mesh,
        in_specs=placed,
        out_specs=(
            P("dp", "ctx", None),
            P("dp", "ctx", None),
            P(None, ("dp", "ctx", "tensor")),
            P(None, ("dp", "ctx"), None, "tensor"),
            P(None, ("dp", "ctx"), "tensor"),
            P(None, ("dp", "ctx", "tensor"), None),
            P(None, "tensor", None),
            P(None, ("dp", "ctx", "tensor"), None),
            P(None, "tensor"),
            P(None, "tensor"),
            P(None, "tensor"),
            P(None, ("dp", "ctx"), "tensor"),
            P(None, ("dp", "ctx", "tensor"), None, None),
            P(None, ("dp", "ctx"), "tensor"),
            P(None, ("dp", "ctx"), "tensor"),
            P(None, ("dp", "ctx", "tensor")),
            P(None, ("dp", "ctx"), None, "tensor"),
            P(None, ("dp", "ctx"), "tensor"),
        ),
        check_vma=False,
    )
```

```python
import jax
import jax.numpy as jnp
from jax import lax
from jax.experimental import pallas as pl
from jax.experimental.pallas import tpu as pltpu
from jax.sharding import PartitionSpec as P

HP = 64
NS = 128
HQ = 8
HK = 2
HD = 64
EPSILON = 1e-05
HIGHEST = lax.Precision.HIGHEST
MASKED = -1e30
F32 = jnp.float32
BF16 = jnp.bfloat16

GATE, QUERY, INNER, STATE, KEYVAL, STEP = 0, 384, 512, 896, 1152, 1280
WIDTH = 1408
EARLY = 512
CONV = 640
ROWS = 256
MESSAGE = 656
VMEM_LIMIT = 20 * 1024 * 1024


def shifted(x, axis, distance):
    count = lax.axis_size(axis)
    route = [(i, i + distance) for i in range(count) if 0 <= i + distance < count]
    return lax.ppermute(x, axis, route)


def swapped(x, distance):
    return lax.ppermute(x, "tensor", [(i, i ^ distance) for i in range(4)])


def chip_sums(mine, other):
    chip = (mine.astype(F32) + swapped(other, 1).astype(F32)).astype(BF16)
    return chip, swapped(chip, 2)


def own_half(x):
    core = lax.axis_index("tensor") & 1
    return lax.dynamic_slice_in_dim(x, core * (x.shape[0] // 2), x.shape[0] // 2, 0)


def both_halves(x):
    core = (lax.axis_index("tensor") & 1).astype(jnp.int32).reshape(1)
    return core, x, swapped(x, 1)


def gather_half(x):
    core = lax.axis_index("tensor") & 1
    other = swapped(x, 1)
    first = jnp.where(core == 0, x, other)
    second = jnp.where(core == 0, other, x)
    return jnp.concatenate([first, second], axis=0)


def mm(a, b):
    return lax.dot_general(a, b, (((1,), (0,)), ((), ())), preferred_element_type=F32)


def mm_t(a, b):
    return lax.dot_general(a, b, (((1,), (1,)), ((), ())), preferred_element_type=F32)


def t_mm(a, b):
    return lax.dot_general(a, b, (((0,), (0,)), ((), ())), preferred_element_type=F32)


def iota(shape, dim):
    return lax.broadcasted_iota(jnp.int32, shape, dim)


def softplus(x):
    return jnp.maximum(x, 0.0) + jnp.log1p(jnp.exp(-jnp.abs(x)))


def sigmoid(x):
    return 1.0 / (1.0 + jnp.exp(-x))


def pair_lanes(columns, j, rows):
    low = iota((rows, 128), 1) < 64
    return jnp.where(low, columns[:, 2 * j : 2 * j + 1], columns[:, 2 * j + 1 : 2 * j + 2])


def pair_sums(values, j, rows):
    low = iota((rows, 128), 1) < 64
    first = jnp.sum(jnp.where(low, values, 0.0), axis=1, keepdims=True)
    second = jnp.sum(jnp.where(low, 0.0, values), axis=1, keepdims=True)
    lane = iota((rows, 128), 1)
    return jnp.where(lane == 2 * j, first, 0.0) + jnp.where(lane == 2 * j + 1, second, 0.0)


def deal_halves(core, full, mine_o, other_o):
    half = ROWS // 2
    mine_o[...] = full[pl.ds(pl.multiple_of(core[0] * half, half), half), :].astype(BF16)
    other_o[...] = full[pl.ds(pl.multiple_of((1 - core[0]) * half, half), half), :].astype(BF16)


def normalise_kernel(one, two, resid, gain, total_o, normed_o):
    total = resid[...] + (one[...].astype(F32) + two[...].astype(F32))
    total_o[...] = total
    scale = lax.rsqrt(jnp.mean(total * total, axis=1, keepdims=True) + EPSILON)
    normed_o[...] = (total * scale * gain[...]).astype(BF16)


def normalise_back_kernel(one, two, x, gain, grad, total_o, low_o):
    values = x[...]
    g = (one[...].astype(F32) + two[...].astype(F32)) * gain[...]
    scale = lax.rsqrt(jnp.mean(values * values, axis=1, keepdims=True) + EPSILON)
    along = jnp.mean(g * values, axis=1, keepdims=True)
    total = grad[...] + (g * scale - values * (scale * scale * scale * along))
    total_o[...] = total
    low_o[...] = total.astype(BF16)


def place_halves(core, own, other, full):
    half = ROWS // 2
    full[pl.ds(pl.multiple_of(core[0] * half, half), half), :] = own[...]
    full[pl.ds(pl.multiple_of((1 - core[0]) * half, half), half), :] = other[...]


def turn(x, cosine, sine):
    lane = iota(x.shape, 1) % 64
    ahead = pltpu.roll(x, 96, 1)
    behind = pltpu.roll(x, 32, 1)
    return x * cosine + jnp.where(lane < 32, -ahead, behind) * sine


def Far(array, layer=None):
    return array if layer is None else array[layer]


def call(kernel, outs, args, scratch=(), after=()):
    after = list(after)
    count = len(args)
    spaces = [pltpu.SMEM if a.dtype == jnp.int32 else pltpu.VMEM for a in args]

    def inner(*refs):
        kernel(*refs[:count], *refs[count + len(after) :])

    return pl.pallas_call(
        inner,
        out_shape=[jax.ShapeDtypeStruct(s, d) for s, d in outs],
        in_specs=[pl.BlockSpec(memory_space=m) for m in spaces]
        + [pl.BlockSpec(memory_space=pl.ANY) for _ in after],
        out_specs=[pl.BlockSpec(memory_space=pltpu.VMEM) for _ in outs],
        scratch_shapes=list(scratch),
        compiler_params=pltpu.CompilerParams(vmem_limit_bytes=VMEM_LIMIT),
        cost_estimate=pl.CostEstimate(flops=10**8, bytes_accessed=10**6, transcendentals=0),
    )(*args, *after)


def project_kernel(
    core, own, other, w_gate, w_q, w_inner, w_bc, w_kv, w_dt, cos, sin,
    normed_o, proj_o, q_o, kv_o, rim_o,
):
    place_halves(core, own, other, normed_o)
    normed = normed_o[...]
    proj_o[:, GATE:QUERY] = mm(normed, w_gate[...])
    proj_o[:, QUERY:INNER] = mm(normed, w_q[...])
    proj_o[:, INNER:STATE] = mm(normed, w_inner[...])
    proj_o[:, STATE:KEYVAL] = mm(normed, w_bc[...])
    proj_o[:, KEYVAL:STEP] = mm(normed, w_kv[...])
    proj_o[:, STEP:WIDTH] = mm(normed, w_dt[...])
    q_o[...] = turn(proj_o[:, QUERY:INNER], cos[...], sin[...]).astype(BF16)
    is_key = iota((ROWS, 128), 1) < 64
    kv = proj_o[:, KEYVAL:STEP]
    kv_o[...] = jnp.where(is_key, turn(kv, cos[...], sin[...]), kv).astype(BF16)
    for j in range(5):
        rim_o[16 * j : 16 * j + 16, :] = proj_o[
            ROWS - 16 : ROWS, INNER + 128 * j : INNER + 128 * j + 128
        ].astype(BF16)


def fill_extended(proj, near, ext):
    for j in range(5):
        at = slice(128 * j, 128 * j + 128)
        ext[0:8, at] = near[16 * j : 16 * j + 16, :].astype(F32)[8:16, :]
    ext[8 : 8 + ROWS, :] = proj[:, INNER:KEYVAL].astype(BF16).astype(F32)


def feed_forward_kernel(
    core, own, other, w_gu, w_down, normed_o, gate_up_o, swiglu_o, mine_o, other_o, full
):
    place_halves(core, own, other, normed_o)
    gate_up_o[...] = mm(normed_o[...], w_gu[...])
    units = swiglu_o.shape[1]
    gate = gate_up_o[:, 0:units]
    swiglu_o[...] = (gate * sigmoid(gate) * gate_up_o[:, units : 2 * units]).astype(BF16)
    full[...] = mm_t(swiglu_o[...], w_down[...])
    deal_halves(core, full, mine_o, other_o)


def ssm_local_kernel(proj, near, kv, kern, heads, colp, segr, pre_o, yloc_o, stepcum_o, msg_o, ext):
    fill_extended(proj, near, ext)
    pre = jnp.zeros((ROWS, CONV), F32)
    for k in range(4):
        pre = pre + ext[5 + k : 5 + k + ROWS, :] * kern[k : k + 1, :] * colp[:, 2 + k : 3 + k]
    pre_o[...] = pre
    act = pre * sigmoid(pre)
    step = softplus(proj[:, STEP:WIDTH] + heads[0:1, :])
    decay = -jnp.exp(heads[1:2, :]) * step
    order = iota((ROWS, ROWS), 0) >= iota((ROWS, ROWS), 1)
    cum = jnp.dot(order.astype(F32), decay, precision=HIGHEST, preferred_element_type=F32)
    stepcum_o[:, 0:128] = step
    stepcum_o[:, 128:256] = cum
    cum_t = cum.T
    same = (colp[:, 0:1] == segr[0:1, 0:ROWS]) & order
    b_low = act[:, 384:512].astype(BF16)
    c_low = act[:, 512:640].astype(BF16)
    scores = mm_t(c_low, b_low)
    last = cum[ROWS - 1 : ROWS, :]
    tail = jnp.where(colp[:, 6:7] > 0.5, jnp.exp(last - cum), 0.0) * step
    low = iota((ROWS, 128), 1) < 64
    for j in range(3):
        tile = act[:, 128 * j : 128 * j + 128]
        scaled = (tile * pair_lanes(step, j, ROWS)).astype(BF16)
        sides = []
        for h in (2 * j, 2 * j + 1):
            gap = jnp.where(same, cum[:, h : h + 1] - cum_t[h : h + 1, :], MASKED)
            sides.append(mm((scores * jnp.exp(gap)).astype(BF16), scaled))
        yloc_o[:, 128 * j : 128 * j + 128] = jnp.where(low, sides[0], sides[1])
        weighted = (tile * pair_lanes(tail, j, ROWS)).astype(BF16)
        msg_o[ROWS + 128 * j : ROWS + 128 * j + 128, :] = t_mm(weighted, b_low).astype(BF16)
    msg_o[0:ROWS, :] = kv[...]
    msg_o[ROWS + 384 : MESSAGE, :] = jnp.broadcast_to(
        jnp.exp(last) * colp[ROWS - 1 : ROWS, 1:2], (16, 128)
    ).astype(BF16)


def chained(m1, m2, m3, out):
    d1 = m1[ROWS + 384 : MESSAGE, :].astype(F32)
    d2 = m2[ROWS + 384 : MESSAGE, :].astype(F32)
    for h in range(6):
        at = slice(ROWS + 64 * h, ROWS + 64 * h + 64)
        inner = m2[at, :].astype(F32) + d2[0:1, h : h + 1] * m3[at, :].astype(F32)
        out[64 * h : 64 * h + 64, :] = m1[at, :].astype(F32) + d1[0:1, h : h + 1] * inner


def mixer_kernel(
    core, proj, pre, yloc, stepcum, m1, m2, m3, heads, colp, att, w_o, w_out,
    state_o, y_o, feat_o, mine_o, other_o, full,
):
    chained(m1, m2, m3, state_o)
    c_pre = pre[:, 512:640]
    c_low = (c_pre * sigmoid(c_pre)).astype(BF16)
    grow = jnp.exp(stepcum[:, 128:256]) * colp[:, 1:2]
    inflow = mm_t(c_low, state_o[...].astype(BF16))
    feat_o[:, 0:128] = att[...]
    for j in range(3):
        at = slice(128 * j, 128 * j + 128)
        y = yloc[:, at] + inflow[:, at] * pair_lanes(grow, j, ROWS)
        y_o[:, at] = y
        x_pre = pre[:, at]
        gate = proj[:, at]
        ssm = y + x_pre * sigmoid(x_pre) * pair_lanes(heads[2:3, :], j, 1)
        feat_o[:, 128 + 128 * j : 256 + 128 * j] = (ssm * gate * sigmoid(gate)).astype(BF16)
    full[...] = mm_t(feat_o[:, 0:128], w_o[...]) + mm_t(feat_o[:, 128:512], w_out[...])
    deal_halves(core, full, mine_o, other_o)


def head_sides(q):
    low = iota(q.shape, 1) < 64
    return (
        jnp.where(low, q, 0.0),
        jnp.where(low, pltpu.roll(q, 64, 1), 0.0),
    )


def attention_kernel(q, kv0, kv1, kv2, kv3, colp, segr, att_o):
    kvs = [r[0:ROWS, :] for r in (kv0, kv1, kv2, kv3)]
    low = iota((ROWS, 128), 1) < 64
    seg_q = colp[:, 0:1]
    order = iota((ROWS, ROWS), 0) >= iota((ROWS, ROWS), 1)
    masks = [seg_q == segr[0:1, ROWS * k : ROWS * k + ROWS] for k in range(4)]
    masks[0] = masks[0] & order
    outs = []
    for side in head_sides(q[...].astype(F32)):
        side = (side * 0.125).astype(BF16)
        scores = [
            jnp.where(masks[k], mm_t(side, kvs[k]), MASKED)
            for k in range(4)
        ]
        top = jnp.max(scores[0], axis=1, keepdims=True)
        for k in range(1, 4):
            top = jnp.maximum(top, jnp.max(scores[k], axis=1, keepdims=True))
        weights = [jnp.exp(s - top) for s in scores]
        total = sum(jnp.sum(w, axis=1, keepdims=True) for w in weights)
        inv = 1.0 / total
        out = jnp.zeros((ROWS, 128), F32)
        for k in range(4):
            out = out + mm((weights[k] * inv).astype(BF16), kvs[k])
        outs.append(out)
    att_o[...] = jnp.where(low, pltpu.roll(outs[0], 64, 1), outs[1]).astype(BF16)


def attention_back_kernel(
    q, kv0, kv1, kv2, kv3, colp, segr, datt, cos, sin, dstate, dq_o, own_o, sent1, sent2, sent3
):
    kvs = [r[0:ROWS, :] for r in (kv0, kv1, kv2, kv3)]
    low = iota((ROWS, 128), 1) < 64
    seg_q = colp[:, 0:1]
    order = iota((ROWS, ROWS), 0) >= iota((ROWS, ROWS), 1)
    masks = [seg_q == segr[0:1, ROWS * k : ROWS * k + ROWS] for k in range(4)]
    masks[0] = masks[0] & order
    d_out = datt[...].astype(F32)
    d_sides = (
        jnp.where(low, 0.0, pltpu.roll(d_out, 64, 1)).astype(BF16),
        jnp.where(low, 0.0, d_out).astype(BF16),
    )
    grads = [jnp.zeros((ROWS, 128), F32) for _ in range(4)]
    dqs = []
    for side, d_side in zip(head_sides(q[...].astype(F32)), d_sides):
        side = (side * 0.125).astype(BF16)
        scores = [
            jnp.where(masks[k], mm_t(side, kvs[k]), MASKED)
            for k in range(4)
        ]
        top = jnp.max(scores[0], axis=1, keepdims=True)
        for k in range(1, 4):
            top = jnp.maximum(top, jnp.max(scores[k], axis=1, keepdims=True))
        weights = [jnp.exp(s - top) for s in scores]
        total = sum(jnp.sum(w, axis=1, keepdims=True) for w in weights)
        inv = 1.0 / total
        probs = [w * inv for w in weights]
        d_probs = [mm_t(d_side, kvs[k]) for k in range(4)]
        inner = sum(jnp.sum(p * d, axis=1, keepdims=True) for p, d in zip(probs, d_probs))
        dq = jnp.zeros((ROWS, 128), F32)
        for k in range(4):
            d_scores = (probs[k] * (d_probs[k] - inner)).astype(BF16)
            dq = dq + mm(d_scores, kvs[k])
            grads[k] = grads[k] + t_mm(d_scores, side) + t_mm(probs[k].astype(BF16), d_side)
        dqs.append(dq * 0.125)
    dq = jnp.where(low, dqs[0], pltpu.roll(dqs[1], 64, 1))
    dq_o[...] = turn(dq, cos[...], -sin[...]).astype(BF16)
    own_o[...] = grads[0]
    for grad, sent in zip(grads[1:], (sent1, sent2, sent3)):
        sent[0:ROWS, :] = grad.astype(BF16)
        sent[ROWS:MESSAGE, :] = dstate[...]


def finish_back_kernel(
    core, own, other, w_o, w_out, proj, pre, y, stepcum, state, heads, colp,
    gm, datt_o, dgate_o, dy_o, dc_o, msg_o, grown,
):
    place_halves(core, own, other, gm)
    datt_o[...] = mm(gm[...], w_o[...]).astype(BF16)
    d_gated = mm(gm[...], w_out[...])
    grow = jnp.exp(stepcum[:, 128:256]) * colp[:, 1:2]
    for j in range(3):
        at = slice(128 * j, 128 * j + 128)
        x_pre = pre[:, at]
        full = y[:, at] + x_pre * sigmoid(x_pre) * pair_lanes(heads[2:3, :], j, 1)
        gate = proj[:, at]
        sig = sigmoid(gate)
        dy = (d_gated[:, at] * gate * sig).astype(BF16)
        dgate_o[:, at] = (d_gated[:, at] * full * sig * (1.0 + gate * (1.0 - sig))).astype(BF16)
        dy_o[:, at] = dy
        grown[:, at] = (dy.astype(F32) * pair_lanes(grow, j, ROWS)).astype(BF16)
    c_pre = pre[:, 512:640]
    c_low = (c_pre * sigmoid(c_pre)).astype(BF16)
    dc_o[...] = mm(grown[...], state[...].astype(BF16))
    msg_o[0:384, :] = t_mm(grown[...], c_low).astype(BF16)
    msg_o[384:400, :] = jnp.broadcast_to(grow[ROWS - 1 : ROWS, :], (16, 128)).astype(BF16)


def ssm_back_kernel(pre, stepcum, dy, dc, colp, segr, dxs_o, db_o, dc_o):
    step = stepcum[:, 0:128]
    cum = stepcum[:, 128:256]
    cum_t = cum.T
    order = iota((ROWS, ROWS), 0) >= iota((ROWS, ROWS), 1)
    same = (colp[:, 0:1] == segr[0:1, 0:ROWS]) & order
    bc = pre[:, 384:640]
    bc = (bc * sigmoid(bc)).astype(BF16)
    b_low, c_low = bc[:, 0:128], bc[:, 128:256]
    scores = mm_t(c_low, b_low)
    d_scores = jnp.zeros((ROWS, ROWS), F32)
    low = iota((ROWS, 128), 1) < 64
    for j in range(3):
        at = slice(128 * j, 128 * j + 128)
        x_pre = pre[:, at]
        scaled = (x_pre * sigmoid(x_pre) * pair_lanes(step, j, ROWS)).astype(BF16)
        dy_low = dy[:, at]
        zero = jnp.zeros_like(dy_low)
        sides = []
        for h in (2 * j, 2 * j + 1):
            decay = jnp.exp(jnp.where(same, cum[:, h : h + 1] - cum_t[h : h + 1, :], MASKED))
            own = jnp.where(low if h == 2 * j else ~low, dy_low, zero)
            d_scores = d_scores + mm_t(own, scaled) * decay
            sides.append(t_mm((scores * decay).astype(BF16), dy_low))
        dxs_o[:, at] = jnp.where(low, sides[0], sides[1])
    d_low = d_scores.astype(BF16)
    db_o[...] = t_mm(d_low, c_low)
    dc_o[...] = dc[...] + mm(d_low, b_low)


def conv_back_kernel(
    proj, near, kern, heads, colp, pre, stepcum, dy, y, dxs, db, dc, state, n1, n2, n3,
    dconv_o, rim_o, dstep_o, small_o, carry, weighted, dact, ext, dext,
):
    chained(n1, n2, n3, carry)
    step = stepcum[:, 0:128]
    cum = stepcum[:, 128:256]
    b_pre = pre[:, 384:512]
    b_low = (b_pre * sigmoid(b_pre)).astype(BF16)
    carry_low = carry[...].astype(BF16)
    spread = mm_t(b_low, carry_low)
    last = cum[ROWS - 1 : ROWS, :]
    tail = jnp.where(colp[:, 6:7] > 0.5, jnp.exp(last - cum), 0.0)
    d_cum = jnp.zeros((ROWS, 128), F32)
    d_step = jnp.zeros((ROWS, 128), F32)
    d_tail = jnp.zeros((ROWS, 128), F32)
    d_skip = jnp.zeros((1, 128), F32)
    for j in range(3):
        at = slice(128 * j, 128 * j + 128)
        x_pre = pre[:, at]
        x = x_pre * sigmoid(x_pre)
        dy_at = dy[:, at].astype(F32)
        step_at = pair_lanes(step, j, ROWS)
        d_scaled = dxs[:, at] + spread[:, at] * pair_lanes(tail, j, ROWS)
        dact[:, at] = d_scaled * step_at + dy_at * pair_lanes(heads[2:3, :], j, 1)
        d_step = d_step + pair_sums(d_scaled * x, j, ROWS)
        weighted[:, at] = (x * pair_lanes(tail * step, j, ROWS)).astype(BF16)
        d_tail = d_tail + pair_sums(weighted[:, at].astype(F32) * spread[:, at], j, ROWS)
        scaled = (x * step_at).astype(BF16).astype(F32)
        d_cum = d_cum + pair_sums(dy_at * y[:, at] - scaled * dxs[:, at], j, ROWS)
        d_skip = d_skip + pair_sums(jnp.sum(dy_at * x, axis=0, keepdims=True), j, 1)
    dact[:, 384:512] = db[...] + mm(weighted[...], carry_low)
    dact[:, 512:640] = dc[...]
    d_cum = d_cum - d_tail
    d_decay = jnp.zeros((1, 128), F32)
    lane = iota((1, 128), 1)
    for h in range(6):
        hs = slice(64 * h, 64 * h + 64)
        d_decay = d_decay + jnp.where(lane == h, jnp.sum(carry[hs, :] * state[hs, :]), 0.0)
    d_last = (
        jnp.sum(d_tail, axis=0, keepdims=True)
        + d_decay * jnp.exp(last) * colp[ROWS - 1 : ROWS, 1:2]
    )
    later = iota((ROWS, ROWS), 0) <= iota((ROWS, ROWS), 1)
    d_log = d_last + jnp.dot(
        later.astype(F32), d_cum, precision=HIGHEST, preferred_element_type=F32
    )
    rate = -jnp.exp(heads[1:2, :])
    d_step = d_step + rate * d_log
    raw = proj[:, STEP:WIDTH] + heads[0:1, :]
    real = iota((ROWS, 128), 1) < 6
    d_raw = jnp.where(real, d_step * sigmoid(raw), 0.0)
    dstep_o[...] = d_raw.astype(BF16)
    small_o[...] = jnp.zeros((32, 128), F32)
    sums = (
        jnp.sum(d_raw, axis=0, keepdims=True),
        jnp.sum(d_log * rate * step, axis=0, keepdims=True),
        d_skip,
    )
    for n, value in enumerate(sums):
        high = value.astype(BF16).astype(F32)
        small_o[20 + n : 21 + n, :] = high
        small_o[23 + n : 24 + n, :] = value - high
    fill_extended(proj, near, ext)
    sig = sigmoid(pre[...])
    d_pre = dact[...] * sig * (1.0 + pre[...] * (1.0 - sig))
    dext[...] = jnp.zeros((8 + ROWS, CONV), F32)
    for k in range(4):
        kept = d_pre * colp[:, 2 + k : 3 + k]
        rows = slice(5 + k, 5 + k + ROWS)
        taps = jnp.sum(ext[rows, :] * kept, axis=0, keepdims=True)
        for j in range(5):
            small_o[5 * k + j : 5 * k + j + 1, :] = taps[:, 128 * j : 128 * j + 128]
        dext[rows, :] = dext[rows, :] + kept * kern[k : k + 1, :]
    rim_o[...] = dext[0:8, :]
    dconv_o[...] = dext[8 : 8 + ROWS, :]


def feed_forward_back_kernel(
    core, own, other, gate_up, w_gu, w_down, normed, gain,
    grad_o, d_gu_o, mine_o, other_o, prod_o, full,
):
    place_halves(core, own, other, grad_o)
    d_swiglu = mm(grad_o[...], w_down[...])
    units = d_swiglu.shape[1]
    gate = gate_up[:, 0:units]
    up = gate_up[:, units : 2 * units]
    sig = sigmoid(gate)
    d_gu_o[:, 0:units] = (d_swiglu * up * sig * (1.0 + gate * (1.0 - sig))).astype(BF16)
    d_gu_o[:, units : 2 * units] = (d_swiglu * gate * sig).astype(BF16)
    part = mm_t(d_gu_o[...], w_gu[...])
    full[...] = part
    deal_halves(core, full, mine_o, other_o)
    prod_o[...] = (part * normed[...].astype(F32) / gain[...]).astype(BF16)


def normed_back_kernel(
    core, dgate, dq, dconv, rim, dkv, k1, k2, k3, dstep, w_gate, w_q, w_inner, w_bc, w_kv, w_dt,
    normed, gain, cos, sin,
    late_o, mine_o, other_o, prod_o, full,
):
    late_o[0 : ROWS - 16, 0:CONV] = dconv[0 : ROWS - 16, :].astype(BF16)
    end = dconv[ROWS - 16 : ROWS, :]
    end = end + jnp.concatenate([jnp.zeros((8, CONV), F32), rim[...]], axis=0)
    late_o[ROWS - 16 : ROWS, 0:CONV] = end.astype(BF16)
    kv = dkv[...]
    for k in (k1, k2, k3):
        kv = kv + k[0:ROWS, :].astype(F32)
    is_key = iota((ROWS, 128), 1) < 64
    kv = jnp.where(is_key, turn(kv, cos[...], -sin[...]), kv)
    late_o[:, CONV : CONV + 128] = kv.astype(BF16)
    part = (
        mm_t(dgate[...], w_gate[...])
        + mm_t(dq[...], w_q[...])
        + mm_t(late_o[:, 0:384], w_inner[...])
        + mm_t(late_o[:, 384:640], w_bc[...])
        + mm_t(late_o[:, 640:768], w_kv[...])
        + mm_t(dstep[...], w_dt[...])
    )
    full[...] = part
    deal_halves(core, full, mine_o, other_o)
    prod_o[...] = (part * normed[...].astype(F32) / gain[...]).astype(BF16)


def row_block(segment, left, extra, at):
    rows = pl.ds(pl.multiple_of(at * 128, 128), 128)
    total = None
    for i, right in segment[0]:
        term = t_mm(left[i][:, rows], right[...])
        total = term if total is None else total + term
    if segment[1]:
        total = jnp.concatenate([extra[...]] * 4, axis=0)
    return total


class Reduction:
    def __init__(self, left, segments, extra=None):
        self.left, self.extra = list(left), extra
        self.terms = [[i for i, _ in seg] for seg in segments]
        self.rights = [r for seg in segments for _, r in seg]
        self.widths = [seg[0][1].shape[1] for seg in segments]
        if extra is not None:
            self.terms.append([])
            self.widths.append(128)
        self.columns = sum(self.widths)
        self.z = (lax.axis_index("dp") % 4).astype(jnp.int32).reshape(1)

    def run(self, kernel, outs, more=(), scratch=(), after=()):
        args = [self.z, *self.left, *self.rights]
        args += [] if self.extra is None else [self.extra]
        count, n_more = len(args), len(more)

        def inner(*refs):
            z, rest = refs[0], refs[1:count]
            left = rest[: len(self.left)]
            rights = list(rest[len(self.left) : len(self.left) + len(self.rights)])
            extra = rest[-1] if self.extra is not None else None
            segments, at = [], 0
            for n, (terms, width) in enumerate(zip(self.terms, self.widths)):
                pairs = [(i, rights.pop(0)) for i in terms]
                last = extra is not None and n == len(self.terms) - 1
                segments.append(((pairs, last), slice(at, at + width)))
                at += width

            def block(dp_hi, offset, columns_done):
                place = dp_hi * 4 + (z[0] + offset) % 4
                for segment, columns in segments:
                    columns_done(columns, row_block(segment, left, extra, place))

            kernel(block, refs[count : count + n_more], refs[count + n_more :])

        return call(inner, outs, (*args, *more), scratch, after)

    def ring(self, x, k):
        route = [(d, (d // 4) * 4 + (d + k) % 4) for d in range(8)]
        return lax.ppermute(x, "dp", route)

    def first(self):
        def kernel(block, _, outs):
            def into(out, rows):
                def done(columns, value):
                    out[rows, columns] = value.astype(BF16)

                return done

            for dp_hi in range(2):
                block(dp_hi, 2, into(outs[dp_hi], slice(0, 128)))
                rows = slice(128 * dp_hi, 128 * dp_hi + 128)
                for offset, out in ((1, outs[2]), (3, outs[3]), (0, outs[4])):
                    block(dp_hi, offset, into(out, rows))

        halves, blocks = ((128, self.columns), BF16), ((256, self.columns), BF16)
        sent = self.run(kernel, [halves] * 2 + [blocks] * 3)
        self.got = (self.ring(sent[0], 1), self.ring(sent[1], -1))
        self.ahead, self.behind, self.own = sent[2:]
        return [sent[4]]

    def second(self):
        low = (self.ahead[:128].astype(F32) + self.got[0].astype(F32)).astype(BF16)
        high = (self.behind[128:].astype(F32) + self.got[1].astype(F32)).astype(BF16)
        ahead = jnp.concatenate([low, self.ahead[128:]], axis=0)
        behind = jnp.concatenate([self.behind[:128], high], axis=0)
        self.got = (self.ring(ahead, 1), self.ring(behind, -1))
        return [ahead, behind]

    def third(self):
        ctx = lax.axis_index("ctx").astype(jnp.int32).reshape(1)

        def kernel(ctx, own, one, two, *refs):
            outs, total = refs[:4], refs[4]
            total[...] = own[...].astype(F32) + (one[...].astype(F32) + two[...].astype(F32))
            for k in range(4):
                for dp_hi in range(2):
                    start = 128 * dp_hi + 32 * ((ctx[0] + k) % 4)
                    piece = total[pl.ds(pl.multiple_of(start, 32), 32), :]
                    outs[k][32 * dp_hi : 32 * dp_hi + 32, :] = piece.astype(BF16)

        outs = call(
            kernel, [((64, self.columns), BF16)] * 4, (ctx, self.own, *self.got),
            [pltpu.VMEM((256, self.columns), F32)],
        )
        routes = [[(i, (i + k) % 4) for i in range(4)] for k in range(4)]
        self.got = [outs[0]] + [lax.ppermute(outs[k], "ctx", routes[k]) for k in (1, 2, 3)]
        return list(outs[1:])

    def fourth(self):
        dp_hi = lax.axis_index("dp") // 4
        total = sum(g.astype(F32) for g in self.got).reshape(2, 32, self.columns)
        mine = lax.dynamic_index_in_dim(total, dp_hi, 0, False)
        other = lax.dynamic_index_in_dim(total, 1 - dp_hi, 0, False).astype(BF16)
        self.got = mine + lax.ppermute(other, "dp", [(d, d ^ 4) for d in range(8)]).astype(F32)
        return [other]


def rms_scale(x):
    return lax.rsqrt(jnp.mean(x * x, axis=-1, keepdims=True) + EPSILON)


def body(
    hidden_in, segments, cotangent, norm_attn, w_zx, w_dt, w_bc, conv_x, conv_bc, dt_bias,
    a_log, d_skip, w_q, w_kv, w_o, w_out, norm_ffn, w_gu, w_down,
):
    layers, width = norm_attn.shape
    rows = hidden_in.shape[1]
    ctx = lax.axis_index("ctx")
    tensor = lax.axis_index("tensor")
    seg_row = segments[0]
    start = ctx * rows
    seg_pad = jnp.concatenate([jnp.full((3 * rows,), -1, jnp.int32), seg_row])
    windows = [
        lax.dynamic_slice_in_dim(seg_pad, start + (3 - k) * rows, rows) for k in range(4)
    ]
    here = windows[0]
    segr = jnp.concatenate(windows).astype(F32)[None]
    near = lax.dynamic_slice_in_dim(seg_pad, start + 3 * rows - 3, rows + 3)
    columns = [here.astype(F32), (here == near[2]).astype(F32)]
    columns += [(near[k : k + rows] == here).astype(F32) for k in range(4)]
    columns += [(here == here[-1]).astype(F32)]
    colp = jnp.pad(jnp.stack(columns, axis=1), ((0, 0), (0, 121)))
    positions = (start + jnp.arange(rows)).astype(F32)
    lane = jnp.arange(128) % 32
    frequency = jnp.exp(-jnp.log(10000.0) * lane.astype(F32) * (2.0 / HD))
    angles = positions[:, None] * frequency[None]
    cos, sin = jnp.cos(angles), jnp.sin(angles)
    kv_head = tensor // 2
    units = w_down.shape[2]

    saved = []
    core = (tensor & 1).astype(jnp.int32).reshape(1)
    half_bf, half_f = ((rows // 2, width), BF16), ((rows // 2, width), F32)
    full_rows = [pltpu.VMEM((rows, width), F32)]
    kernels = jnp.swapaxes(jnp.concatenate([conv_x, conv_bc], axis=1).astype(F32), 1, 2)
    w_dt_wide = jnp.pad(w_dt, ((0, 0), (0, 0), (0, 122)))
    full = hidden_in[0].astype(F32)
    resid = own_half(full)
    for l in range(layers):
        kv_w = lax.dynamic_slice_in_dim(w_kv[l], kv_head * HD, HD, axis=2).reshape(width, 2 * HD)
        w_zx_l, w_gu_l = w_zx[l], w_gu[l]
        if l > 0:
            w_zx_l, w_gu_l, _ = lax.optimization_barrier((w_zx_l, w_gu_l, saved[0]["proj"]))
        w_in = (
            w_zx_l[:, 0], Far(w_q, l), w_zx_l[:, 1], Far(w_bc, l), kv_w, Far(w_dt_wide, l)
        )
        gate_up_w = w_gu_l.reshape(width, -1)
        kern = Far(kernels, l)
        heads = jnp.pad(
            jnp.stack([dt_bias[l], a_log[l], d_skip[l]]), ((0, 5), (0, 122))
        )
        gain_attn = norm_attn[l].astype(F32)[None]
        gain_ffn = norm_ffn[l].astype(F32)[None]
        if l == 0:
            normed = (full * rms_scale(full) * gain_attn).astype(BF16)
            halves = normed.reshape(2, rows // 2, width)
            parts = [lax.dynamic_index_in_dim(halves, i, 0, False) for i in (core[0], 1 - core[0])]
            halves = (core, *parts)
        else:
            halves = both_halves(low)
        normed, proj, q, kv, rim = call(
            project_kernel,
            [((rows, width), BF16), ((rows, WIDTH), F32), ((rows, 128), BF16),
             ((rows, 128), BF16), ((80, 128), BF16)],
            (*halves, *w_in, cos, sin),
        )
        rim = shifted(rim, "ctx", 1)
        pre, yloc, stepcum, msg = call(
            ssm_local_kernel,
            [((rows, CONV), F32), ((rows, 384), F32), ((rows, 256), F32), ((MESSAGE, 128), BF16)],
            (proj, rim, kv, kern, heads, colp, segr),
            [pltpu.VMEM((8 + ROWS, CONV), F32)],
        )
        states = [shifted(msg, "ctx", k) for k in (1, 2, 3)]
        kvs = (msg, *states)
        (att,) = call(attention_kernel, [((rows, 128), BF16)], (q, *kvs, colp, segr))
        state, y, feat, *mixer = call(
            mixer_kernel,
            [((384, 128), F32), ((rows, 384), F32), ((rows, 512), BF16), half_bf, half_bf],
            (core, proj, pre, yloc, stepcum, *states, heads, colp, att, Far(w_o, l), Far(w_out, l)),
            full_rows,
        )
        hidden, low = call(
            normalise_kernel, [half_f, half_bf], (*chip_sums(*mixer), resid, gain_ffn)
        )
        normed_ffn, gate_up, swiglu, *ffn = call(
            feed_forward_kernel,
            [((rows, width), BF16), ((rows, 2 * units), F32), ((rows, units), BF16),
             half_bf, half_bf],
            (*both_halves(low), gate_up_w, Far(w_down, l)),
            full_rows,
        )
        saved.append(
            dict(
                w_in=w_in, gate_up_w=gate_up_w, kern=kern, heads=heads, gain_attn=gain_attn,
                gain_ffn=gain_ffn, resid=resid, normed=normed, proj=proj, q=q, kvs=kvs, rim=rim,
                pre=pre, stepcum=stepcum, state=state, y=y, feat=feat, hidden=hidden,
                normed_ffn=normed_ffn, gate_up=gate_up, swiglu=swiglu,
            )
        )
        if l + 1 < layers:
            resid, low = call(
                normalise_kernel, [half_f, half_bf],
                (*chip_sums(*ffn), hidden, norm_attn[l + 1].astype(F32)[None]),
            )
    one, two = chip_sums(*ffn)
    out = gather_half((hidden + (one.astype(F32) + two.astype(F32))).astype(BF16))

    grad = own_half(cotangent[0])
    grad_low = grad.astype(BF16)
    lane = jnp.arange(128)
    hot = [jnp.broadcast_to((lane == n).astype(BF16), (rows, 128)) for n in (6, 7)]
    owned = [None] * layers
    pins = []
    for l in reversed(range(layers)):
        s = saved[l]
        grad_ffn, d_gu, *part, prod_ffn = call(
            feed_forward_back_kernel,
            [((rows, width), BF16), ((rows, 2 * units), BF16), half_bf, half_bf,
             ((rows, width), BF16)],
            (*both_halves(grad_low), Far(s["gate_up"]), Far(s["gate_up_w"]), Far(w_down, l),
             Far(s["normed_ffn"]), s["gain_ffn"]),
            full_rows,
            pins,
        )
        group_ffn = Reduction(
            (Far(s["normed_ffn"]), grad_ffn), [[(0, d_gu)], [(1, Far(s["swiglu"]))]]
        )
        pins = group_ffn.first()
        if l < layers - 1:
            pins += group_ffn_up.fourth() + group_mix.second()
        grad_hidden, low = call(
            normalise_back_kernel, [half_f, half_bf],
            (*chip_sums(*part), Far(s["hidden"]), s["gain_ffn"], grad),
        )
        gm, datt, dgate, dy, dc, msg = call(
            finish_back_kernel,
            [
                ((rows, width), BF16), ((rows, 128), BF16), ((rows, 384), BF16),
                ((rows, 384), BF16), ((rows, 128), F32), ((400, 128), BF16),
            ],
            (*both_halves(low), Far(w_o, l), Far(w_out, l), Far(s["proj"]),
             Far(s["pre"]), Far(s["y"]), Far(s["stepcum"]), Far(s["state"]), Far(s["heads"]), Far(colp)),
            [pltpu.VMEM((ROWS, 384), BF16)],
            pins,
        )
        dq, dkv_own, *sents = call(
            attention_back_kernel,
            [((rows, 128), BF16), ((rows, 128), F32)] + [((MESSAGE, 128), BF16)] * 3,
            (Far(s["q"]), *(Far(k) for k in s["kvs"]), Far(colp), Far(segr), datt, Far(cos), Far(sin), msg),
        )
        carries = [shifted(sents[k - 1], "ctx", -k) for k in (1, 2, 3)]
        pins = group_ffn.second()
        if l < layers - 1:
            pins += group_mix.third()
            group_mid = Reduction(
                (Far(s["normed"]), gm), [[(0, dgate)], [(0, dq)], [(1, Far(s["feat"]))]]
            )
            pins += group_mid.first()
        dxs, db, dc = call(
            ssm_back_kernel,
            [((rows, 384), F32), ((rows, 128), F32), ((rows, 128), F32)],
            (Far(s["pre"]), Far(s["stepcum"]), dy, dc, Far(colp), Far(segr)),
        )
        dconv, rim, dstep, small = call(
            conv_back_kernel,
            [((rows, CONV), F32), ((8, CONV), F32), ((rows, 128), BF16), ((32, 128), F32)],
            (Far(s["proj"]), Far(s["rim"]), s["kern"], Far(s["heads"]), Far(colp), Far(s["pre"]),
             Far(s["stepcum"]), dy, Far(s["y"]), dxs, db, dc, Far(s["state"]), *carries),
            [
                pltpu.VMEM((384, 128), F32), pltpu.VMEM((ROWS, 384), BF16),
                pltpu.VMEM((ROWS, CONV), F32), pltpu.VMEM((8 + ROWS, CONV), F32),
                pltpu.VMEM((8 + ROWS, CONV), F32),
            ],
            pins,
        )
        pins = []
        if l < layers - 1:
            pins = group_mix.fourth()
        extra = small
        rim_got = shifted(rim, "ctx", -1)
        late, *part, prod_attn = call(
            normed_back_kernel,
            [((rows, 768), BF16), half_bf, half_bf, ((rows, width), BF16)],
            (core, dgate, dq, dconv, rim_got, dkv_own, *carries, dstep, *s["w_in"], Far(s["normed"]),
             s["gain_attn"], Far(cos), Far(sin)),
            full_rows,
            pins,
        )
        late_cols = [
            [(0, late)],
            [(0, dstep), (1, hot[0]), (2, hot[1])],
        ]
        mix_left = (Far(s["normed"]), prod_attn, prod_ffn)
        if l > 0:
            mid_cols = [[(0, dgate)], [(0, dq)], [(3, Far(s["feat"]))]]
            group_mix = Reduction((*mix_left, gm), mid_cols + late_cols, extra)
            pins = group_ffn.third() + group_mix.first()
            group_ffn_up = group_ffn
            owned[l] = (group_ffn, group_mix)
        else:
            group_late = Reduction(mix_left, late_cols, extra)
            group_late.first()
            group_mid.second()
            group_ffn.third()
            group_late.second()
            group_mid.third()
            group_ffn.fourth()
            group_late.third()
            group_mid.fourth()
            group_late.fourth()
            owned[l] = (group_ffn, group_mid, group_late)
        grad, grad_low = call(
            normalise_back_kernel, [half_f, half_bf],
            (*chip_sums(*part), Far(s["resid"]), s["gain_attn"], grad_hidden),
        )
    grad_hidden_in = gather_half(grad)

    everything = jnp.stack([jnp.concatenate([g.got for g in o], axis=1) for o in owned])
    ffn, mid, late = everything[..., :1536], everything[..., 1536:2560], everything[..., 2560:]
    tile = late[:, :, 896:]
    taps = tile[:, :20].reshape(layers, 4, CONV)
    sums = (tile[:, 20:23] + tile[:, 23:26])[..., :6]
    index = lax.axis_index("dp") * 4 + ctx
    state = lax.dynamic_slice_in_dim(taps[..., 384:], index * 8, 8, 2)
    state = jnp.pad(jnp.swapaxes(state, 1, 2).reshape(layers, 32, 1), ((0, 0), (0, 0), (0, 119)))
    shared = jnp.concatenate([late[:, :, 384:776], state], axis=2)
    shared = jnp.moveaxis(shared.reshape(layers, 4, -1, 512), 1, 0)
    shared = lax.all_to_all(shared, "tensor", 0, 0, tiled=True)
    total = jnp.sum(shared, axis=0)
    head_kv = [jnp.sum(shared[2 * k : 2 * k + 2, ..., 256:384], axis=0) for k in range(2)]
    head_kv = [h.reshape(*h.shape[:-1], 2, HD) for h in head_kv]
    return (
        out[None],
        grad_hidden_in[None],
        total[..., 390],
        jnp.stack([mid[..., :384], late[..., :384]], axis=2),
        late[..., 768:774],
        total[..., :256],
        jnp.swapaxes(taps[..., :384], 1, 2),
        total[..., 392].reshape(layers, 2, 4),
        sums[:, 0],
        sums[:, 1],
        sums[:, 2],
        mid[..., 384:512],
        jnp.concatenate(head_kv, axis=-1),
        mid[..., 512:640],
        mid[..., 640:1024],
        total[..., 391],
        ffn[..., : 2 * units].reshape(layers, -1, 2, units),
        ffn[..., 2 * units :],
    )


def solution(mesh):
    placed = (
        P("dp", "ctx", None),
        P("dp", None),
        P("dp", "ctx", None),
        P(),
        P(None, None, None, "tensor"),
        P(None, None, "tensor"),
        P(),
        P(None, "tensor", None),
        P(),
        P(None, "tensor"),
        P(None, "tensor"),
        P(None, "tensor"),
        P(None, None, "tensor"),
        P(),
        P(None, None, "tensor"),
        P(None, None, "tensor"),
        P(),
        P(None, None, None, "tensor"),
        P(None, None, "tensor"),
    )
    return jax.shard_map(
        body,
        mesh=mesh,
        in_specs=placed,
        out_specs=(
            P("dp", "ctx", None),
            P("dp", "ctx", None),
            P(None, ("dp", "ctx", "tensor")),
            P(None, ("dp", "ctx"), None, "tensor"),
            P(None, ("dp", "ctx"), "tensor"),
            P(None, ("dp", "ctx", "tensor"), None),
            P(None, "tensor", None),
            P(None, ("dp", "ctx", "tensor"), None),
            P(None, "tensor"),
            P(None, "tensor"),
            P(None, "tensor"),
            P(None, ("dp", "ctx"), "tensor"),
            P(None, ("dp", "ctx", "tensor"), None, None),
            P(None, ("dp", "ctx"), "tensor"),
            P(None, ("dp", "ctx"), "tensor"),
            P(None, ("dp", "ctx", "tensor")),
            P(None, ("dp", "ctx"), None, "tensor"),
            P(None, ("dp", "ctx"), "tensor"),
        ),
        check_vma=False,
    )
```

```python
import jax
import jax.numpy as jnp
from jax import lax
from jax.experimental import pallas as pl
from jax.experimental.pallas import tpu as pltpu
from jax.sharding import PartitionSpec as P

HP = 64
NS = 128
HQ = 8
HK = 2
HD = 64
EPSILON = 1e-05
HIGHEST = lax.Precision.HIGHEST
MASKED = -1e30
F32 = jnp.float32
BF16 = jnp.bfloat16

GATE, QUERY, INNER, STATE, KEYVAL, STEP = 0, 384, 512, 896, 1152, 1280
WIDTH = 1408
EARLY = 512
CONV = 640
ROWS = 256
MESSAGE = 656
VMEM_LIMIT = 20 * 1024 * 1024


def shifted(x, axis, distance):
    count = lax.axis_size(axis)
    route = [(i, i + distance) for i in range(count) if 0 <= i + distance < count]
    return lax.ppermute(x, axis, route)


def swapped(x, distance):
    return lax.ppermute(x, "tensor", [(i, i ^ distance) for i in range(4)])


def chip_sums(mine, other):
    chip = (mine.astype(F32) + swapped(other, 1).astype(F32)).astype(BF16)
    return chip, swapped(chip, 2)


def own_half(x):
    core = lax.axis_index("tensor") & 1
    return lax.dynamic_slice_in_dim(x, core * (x.shape[0] // 2), x.shape[0] // 2, 0)


def both_halves(x):
    core = (lax.axis_index("tensor") & 1).astype(jnp.int32).reshape(1)
    return core, x, swapped(x, 1)


def gather_half(x):
    core = lax.axis_index("tensor") & 1
    other = swapped(x, 1)
    first = jnp.where(core == 0, x, other)
    second = jnp.where(core == 0, other, x)
    return jnp.concatenate([first, second], axis=0)


def mm(a, b):
    return lax.dot_general(a, b, (((1,), (0,)), ((), ())), preferred_element_type=F32)


def mm_t(a, b):
    return lax.dot_general(a, b, (((1,), (1,)), ((), ())), preferred_element_type=F32)


def t_mm(a, b):
    return lax.dot_general(a, b, (((0,), (0,)), ((), ())), preferred_element_type=F32)


def iota(shape, dim):
    return lax.broadcasted_iota(jnp.int32, shape, dim)


def softplus(x):
    return jnp.maximum(x, 0.0) + jnp.log1p(jnp.exp(-jnp.abs(x)))


def sigmoid(x):
    return 1.0 / (1.0 + jnp.exp(-x))


def pair_lanes(columns, j, rows):
    low = iota((rows, 128), 1) < 64
    return jnp.where(low, columns[:, 2 * j : 2 * j + 1], columns[:, 2 * j + 1 : 2 * j + 2])


def pair_sums(values, j, rows):
    low = iota((rows, 128), 1) < 64
    first = jnp.sum(jnp.where(low, values, 0.0), axis=1, keepdims=True)
    second = jnp.sum(jnp.where(low, 0.0, values), axis=1, keepdims=True)
    lane = iota((rows, 128), 1)
    return jnp.where(lane == 2 * j, first, 0.0) + jnp.where(lane == 2 * j + 1, second, 0.0)


def deal_halves(core, full, mine_o, other_o):
    half = ROWS // 2
    mine_o[...] = full[pl.ds(pl.multiple_of(core[0] * half, half), half), :].astype(BF16)
    other_o[...] = full[pl.ds(pl.multiple_of((1 - core[0]) * half, half), half), :].astype(BF16)


def normalise_kernel(one, two, resid, gain, total_o, normed_o):
    total = resid[...] + (one[...].astype(F32) + two[...].astype(F32))
    total_o[...] = total
    scale = lax.rsqrt(jnp.mean(total * total, axis=1, keepdims=True) + EPSILON)
    normed_o[...] = (total * scale * gain[...]).astype(BF16)


def normalise_back_kernel(one, two, x, gain, grad, total_o, low_o):
    values = x[...]
    g = (one[...].astype(F32) + two[...].astype(F32)) * gain[...]
    scale = lax.rsqrt(jnp.mean(values * values, axis=1, keepdims=True) + EPSILON)
    along = jnp.mean(g * values, axis=1, keepdims=True)
    total = grad[...] + (g * scale - values * (scale * scale * scale * along))
    total_o[...] = total
    low_o[...] = total.astype(BF16)


def place_halves(core, own, other, full):
    half = ROWS // 2
    full[pl.ds(pl.multiple_of(core[0] * half, half), half), :] = own[...]
    full[pl.ds(pl.multiple_of((1 - core[0]) * half, half), half), :] = other[...]


def turn(x, cosine, sine):
    lane = iota(x.shape, 1) % 64
    ahead = pltpu.roll(x, 96, 1)
    behind = pltpu.roll(x, 32, 1)
    return x * cosine + jnp.where(lane < 32, -ahead, behind) * sine


def Far(array, layer=None):
    return array if layer is None else array[layer]


def call(kernel, outs, args, scratch=(), after=()):
    after = list(after)
    count = len(args)
    spaces = [pltpu.SMEM if a.dtype == jnp.int32 else pltpu.VMEM for a in args]

    def inner(*refs):
        kernel(*refs[:count], *refs[count + len(after) :])

    return pl.pallas_call(
        inner,
        out_shape=[jax.ShapeDtypeStruct(s, d) for s, d in outs],
        in_specs=[pl.BlockSpec(memory_space=m) for m in spaces]
        + [pl.BlockSpec(memory_space=pl.ANY) for _ in after],
        out_specs=[pl.BlockSpec(memory_space=pltpu.VMEM) for _ in outs],
        scratch_shapes=list(scratch),
        compiler_params=pltpu.CompilerParams(vmem_limit_bytes=VMEM_LIMIT),
        cost_estimate=pl.CostEstimate(flops=10**8, bytes_accessed=10**6, transcendentals=0),
    )(*args, *after)


def project_kernel(
    core, own, other, w_gate, w_q, w_inner, w_bc, w_kv, w_dt, cos, sin,
    normed_o, proj_o, q_o, kv_o, rim_o,
):
    place_halves(core, own, other, normed_o)
    normed = normed_o[...]
    proj_o[:, GATE:QUERY] = mm(normed, w_gate[...])
    proj_o[:, QUERY:INNER] = mm(normed, w_q[...])
    proj_o[:, INNER:STATE] = mm(normed, w_inner[...])
    proj_o[:, STATE:KEYVAL] = mm(normed, w_bc[...])
    proj_o[:, KEYVAL:STEP] = mm(normed, w_kv[...])
    proj_o[:, STEP:WIDTH] = mm(normed, w_dt[...])
    q_o[...] = turn(proj_o[:, QUERY:INNER], cos[...], sin[...]).astype(BF16)
    is_key = iota((ROWS, 128), 1) < 64
    kv = proj_o[:, KEYVAL:STEP]
    kv_o[...] = jnp.where(is_key, turn(kv, cos[...], sin[...]), kv).astype(BF16)
    for j in range(5):
        rim_o[16 * j : 16 * j + 16, :] = proj_o[
            ROWS - 16 : ROWS, INNER + 128 * j : INNER + 128 * j + 128
        ].astype(BF16)


def fill_extended(proj, near, ext):
    for j in range(5):
        at = slice(128 * j, 128 * j + 128)
        ext[0:8, at] = near[16 * j : 16 * j + 16, :].astype(F32)[8:16, :]
    ext[8 : 8 + ROWS, :] = proj[:, INNER:KEYVAL].astype(BF16).astype(F32)


def feed_forward_kernel(
    core, own, other, w_gu, w_down, normed_o, gate_up_o, swiglu_o, mine_o, other_o, full
):
    place_halves(core, own, other, normed_o)
    gate_up_o[...] = mm(normed_o[...], w_gu[...])
    units = swiglu_o.shape[1]
    gate = gate_up_o[:, 0:units]
    swiglu_o[...] = (gate * sigmoid(gate) * gate_up_o[:, units : 2 * units]).astype(BF16)
    full[...] = mm_t(swiglu_o[...], w_down[...])
    deal_halves(core, full, mine_o, other_o)


def ssm_local_kernel(proj, near, kv, kern, heads, colp, segr, pre_o, yloc_o, stepcum_o, msg_o, ext):
    fill_extended(proj, near, ext)
    pre = jnp.zeros((ROWS, CONV), F32)
    for k in range(4):
        pre = pre + ext[5 + k : 5 + k + ROWS, :] * kern[k : k + 1, :] * colp[:, 2 + k : 3 + k]
    pre_o[...] = pre
    act = pre * sigmoid(pre)
    step = softplus(proj[:, STEP:WIDTH] + heads[0:1, :])
    decay = -jnp.exp(heads[1:2, :]) * step
    order = iota((ROWS, ROWS), 0) >= iota((ROWS, ROWS), 1)
    cum = jnp.dot(order.astype(F32), decay, precision=HIGHEST, preferred_element_type=F32)
    stepcum_o[:, 0:128] = step
    stepcum_o[:, 128:256] = cum
    cum_t = cum.T
    same = (colp[:, 0:1] == segr[0:1, 0:ROWS]) & order
    b_low = act[:, 384:512].astype(BF16)
    c_low = act[:, 512:640].astype(BF16)
    scores = mm_t(c_low, b_low)
    last = cum[ROWS - 1 : ROWS, :]
    tail = jnp.where(colp[:, 6:7] > 0.5, jnp.exp(last - cum), 0.0) * step
    low = iota((ROWS, 128), 1) < 64
    for j in range(3):
        tile = act[:, 128 * j : 128 * j + 128]
        scaled = (tile * pair_lanes(step, j, ROWS)).astype(BF16)
        sides = []
        for h in (2 * j, 2 * j + 1):
            gap = jnp.where(same, cum[:, h : h + 1] - cum_t[h : h + 1, :], MASKED)
            sides.append(mm((scores * jnp.exp(gap)).astype(BF16), scaled))
        yloc_o[:, 128 * j : 128 * j + 128] = jnp.where(low, sides[0], sides[1])
        weighted = (tile * pair_lanes(tail, j, ROWS)).astype(BF16)
        msg_o[ROWS + 128 * j : ROWS + 128 * j + 128, :] = t_mm(weighted, b_low).astype(BF16)
    msg_o[0:ROWS, :] = kv[...]
    msg_o[ROWS + 384 : MESSAGE, :] = jnp.broadcast_to(
        jnp.exp(last) * colp[ROWS - 1 : ROWS, 1:2], (16, 128)
    ).astype(BF16)


def chained(m1, m2, m3, out):
    d1 = m1[ROWS + 384 : MESSAGE, :].astype(F32)
    d2 = m2[ROWS + 384 : MESSAGE, :].astype(F32)
    for h in range(6):
        at = slice(ROWS + 64 * h, ROWS + 64 * h + 64)
        inner = m2[at, :].astype(F32) + d2[0:1, h : h + 1] * m3[at, :].astype(F32)
        out[64 * h : 64 * h + 64, :] = m1[at, :].astype(F32) + d1[0:1, h : h + 1] * inner


def mixer_kernel(
    core, proj, pre, yloc, stepcum, m1, m2, m3, heads, colp, att, w_o, w_out,
    state_o, y_o, feat_o, mine_o, other_o, full,
):
    chained(m1, m2, m3, state_o)
    c_pre = pre[:, 512:640]
    c_low = (c_pre * sigmoid(c_pre)).astype(BF16)
    grow = jnp.exp(stepcum[:, 128:256]) * colp[:, 1:2]
    inflow = mm_t(c_low, state_o[...].astype(BF16))
    feat_o[:, 0:128] = att[...]
    for j in range(3):
        at = slice(128 * j, 128 * j + 128)
        y = yloc[:, at] + inflow[:, at] * pair_lanes(grow, j, ROWS)
        y_o[:, at] = y
        x_pre = pre[:, at]
        gate = proj[:, at]
        ssm = y + x_pre * sigmoid(x_pre) * pair_lanes(heads[2:3, :], j, 1)
        feat_o[:, 128 + 128 * j : 256 + 128 * j] = (ssm * gate * sigmoid(gate)).astype(BF16)
    full[...] = mm_t(feat_o[:, 0:128], w_o[...]) + mm_t(feat_o[:, 128:512], w_out[...])
    deal_halves(core, full, mine_o, other_o)


def head_sides(q):
    low = iota(q.shape, 1) < 64
    return (
        jnp.where(low, q, 0.0),
        jnp.where(low, pltpu.roll(q, 64, 1), 0.0),
    )


def attention_kernel(q, kv0, kv1, kv2, kv3, colp, segr, att_o):
    kvs = [r[0:ROWS, :] for r in (kv0, kv1, kv2, kv3)]
    low = iota((ROWS, 128), 1) < 64
    seg_q = colp[:, 0:1]
    order = iota((ROWS, ROWS), 0) >= iota((ROWS, ROWS), 1)
    masks = [seg_q == segr[0:1, ROWS * k : ROWS * k + ROWS] for k in range(4)]
    masks[0] = masks[0] & order
    outs = []
    for side in head_sides(q[...].astype(F32)):
        side = (side * 0.125).astype(BF16)
        scores = [
            jnp.where(masks[k], mm_t(side, kvs[k]), MASKED)
            for k in range(4)
        ]
        top = jnp.max(scores[0], axis=1, keepdims=True)
        for k in range(1, 4):
            top = jnp.maximum(top, jnp.max(scores[k], axis=1, keepdims=True))
        weights = [jnp.exp(s - top) for s in scores]
        total = sum(jnp.sum(w, axis=1, keepdims=True) for w in weights)
        inv = 1.0 / total
        out = jnp.zeros((ROWS, 128), F32)
        for k in range(4):
            out = out + mm((weights[k] * inv).astype(BF16), kvs[k])
        outs.append(out)
    att_o[...] = jnp.where(low, pltpu.roll(outs[0], 64, 1), outs[1]).astype(BF16)


def attention_back_kernel(
    q, kv0, kv1, kv2, kv3, colp, segr, datt, cos, sin, dstate, dq_o, own_o, sent1, sent2, sent3
):
    kvs = [r[0:ROWS, :] for r in (kv0, kv1, kv2, kv3)]
    low = iota((ROWS, 128), 1) < 64
    seg_q = colp[:, 0:1]
    order = iota((ROWS, ROWS), 0) >= iota((ROWS, ROWS), 1)
    masks = [seg_q == segr[0:1, ROWS * k : ROWS * k + ROWS] for k in range(4)]
    masks[0] = masks[0] & order
    d_out = datt[...].astype(F32)
    d_sides = (
        jnp.where(low, 0.0, pltpu.roll(d_out, 64, 1)).astype(BF16),
        jnp.where(low, 0.0, d_out).astype(BF16),
    )
    grads = [jnp.zeros((ROWS, 128), F32) for _ in range(4)]
    dqs = []
    for side, d_side in zip(head_sides(q[...].astype(F32)), d_sides):
        side = (side * 0.125).astype(BF16)
        scores = [
            jnp.where(masks[k], mm_t(side, kvs[k]), MASKED)
            for k in range(4)
        ]
        top = jnp.max(scores[0], axis=1, keepdims=True)
        for k in range(1, 4):
            top = jnp.maximum(top, jnp.max(scores[k], axis=1, keepdims=True))
        weights = [jnp.exp(s - top) for s in scores]
        total = sum(jnp.sum(w, axis=1, keepdims=True) for w in weights)
        inv = 1.0 / total
        probs = [w * inv for w in weights]
        d_probs = [mm_t(d_side, kvs[k]) for k in range(4)]
        inner = sum(jnp.sum(p * d, axis=1, keepdims=True) for p, d in zip(probs, d_probs))
        dq = jnp.zeros((ROWS, 128), F32)
        for k in range(4):
            d_scores = (probs[k] * (d_probs[k] - inner)).astype(BF16)
            dq = dq + mm(d_scores, kvs[k])
            grads[k] = grads[k] + t_mm(d_scores, side) + t_mm(probs[k].astype(BF16), d_side)
        dqs.append(dq * 0.125)
    dq = jnp.where(low, dqs[0], pltpu.roll(dqs[1], 64, 1))
    dq_o[...] = turn(dq, cos[...], -sin[...]).astype(BF16)
    own_o[...] = grads[0]
    for grad, sent in zip(grads[1:], (sent1, sent2, sent3)):
        sent[0:ROWS, :] = grad.astype(BF16)
        sent[ROWS:MESSAGE, :] = dstate[...]


def finish_back_kernel(
    core, own, other, w_o, w_out, proj, pre, y, stepcum, state, heads, colp,
    gm, datt_o, dgate_o, dy_o, dc_o, msg_o, grown,
):
    place_halves(core, own, other, gm)
    datt_o[...] = mm(gm[...], w_o[...]).astype(BF16)
    d_gated = mm(gm[...], w_out[...])
    grow = jnp.exp(stepcum[:, 128:256]) * colp[:, 1:2]
    for j in range(3):
        at = slice(128 * j, 128 * j + 128)
        x_pre = pre[:, at]
        full = y[:, at] + x_pre * sigmoid(x_pre) * pair_lanes(heads[2:3, :], j, 1)
        gate = proj[:, at]
        sig = sigmoid(gate)
        dy = (d_gated[:, at] * gate * sig).astype(BF16)
        dgate_o[:, at] = (d_gated[:, at] * full * sig * (1.0 + gate * (1.0 - sig))).astype(BF16)
        dy_o[:, at] = dy
        grown[:, at] = (dy.astype(F32) * pair_lanes(grow, j, ROWS)).astype(BF16)
    c_pre = pre[:, 512:640]
    c_low = (c_pre * sigmoid(c_pre)).astype(BF16)
    dc_o[...] = mm(grown[...], state[...].astype(BF16))
    msg_o[0:384, :] = t_mm(grown[...], c_low).astype(BF16)
    msg_o[384:400, :] = jnp.broadcast_to(grow[ROWS - 1 : ROWS, :], (16, 128)).astype(BF16)


def ssm_back_kernel(pre, stepcum, dy, dc, colp, segr, dxs_o, db_o, dc_o):
    step = stepcum[:, 0:128]
    cum = stepcum[:, 128:256]
    cum_t = cum.T
    order = iota((ROWS, ROWS), 0) >= iota((ROWS, ROWS), 1)
    same = (colp[:, 0:1] == segr[0:1, 0:ROWS]) & order
    bc = pre[:, 384:640]
    bc = (bc * sigmoid(bc)).astype(BF16)
    b_low, c_low = bc[:, 0:128], bc[:, 128:256]
    scores = mm_t(c_low, b_low)
    d_scores = jnp.zeros((ROWS, ROWS), F32)
    low = iota((ROWS, 128), 1) < 64
    for j in range(3):
        at = slice(128 * j, 128 * j + 128)
        x_pre = pre[:, at]
        scaled = (x_pre * sigmoid(x_pre) * pair_lanes(step, j, ROWS)).astype(BF16)
        dy_low = dy[:, at]
        zero = jnp.zeros_like(dy_low)
        sides = []
        for h in (2 * j, 2 * j + 1):
            decay = jnp.exp(jnp.where(same, cum[:, h : h + 1] - cum_t[h : h + 1, :], MASKED))
            own = jnp.where(low if h == 2 * j else ~low, dy_low, zero)
            d_scores = d_scores + mm_t(own, scaled) * decay
            sides.append(t_mm((scores * decay).astype(BF16), dy_low))
        dxs_o[:, at] = jnp.where(low, sides[0], sides[1])
    d_low = d_scores.astype(BF16)
    db_o[...] = t_mm(d_low, c_low)
    dc_o[...] = dc[...] + mm(d_low, b_low)


def conv_back_kernel(
    proj, near, kern, heads, colp, pre, stepcum, dy, y, dxs, db, dc, state, n1, n2, n3,
    dconv_o, rim_o, dstep_o, small_o, carry, weighted, dact, ext, dext,
):
    chained(n1, n2, n3, carry)
    step = stepcum[:, 0:128]
    cum = stepcum[:, 128:256]
    b_pre = pre[:, 384:512]
    b_low = (b_pre * sigmoid(b_pre)).astype(BF16)
    carry_low = carry[...].astype(BF16)
    spread = mm_t(b_low, carry_low)
    last = cum[ROWS - 1 : ROWS, :]
    tail = jnp.where(colp[:, 6:7] > 0.5, jnp.exp(last - cum), 0.0)
    d_cum = jnp.zeros((ROWS, 128), F32)
    d_step = jnp.zeros((ROWS, 128), F32)
    d_tail = jnp.zeros((ROWS, 128), F32)
    d_skip = jnp.zeros((1, 128), F32)
    for j in range(3):
        at = slice(128 * j, 128 * j + 128)
        x_pre = pre[:, at]
        x = x_pre * sigmoid(x_pre)
        dy_at = dy[:, at].astype(F32)
        step_at = pair_lanes(step, j, ROWS)
        d_scaled = dxs[:, at] + spread[:, at] * pair_lanes(tail, j, ROWS)
        dact[:, at] = d_scaled * step_at + dy_at * pair_lanes(heads[2:3, :], j, 1)
        d_step = d_step + pair_sums(d_scaled * x, j, ROWS)
        weighted[:, at] = (x * pair_lanes(tail * step, j, ROWS)).astype(BF16)
        d_tail = d_tail + pair_sums(weighted[:, at].astype(F32) * spread[:, at], j, ROWS)
        scaled = (x * step_at).astype(BF16).astype(F32)
        d_cum = d_cum + pair_sums(dy_at * y[:, at] - scaled * dxs[:, at], j, ROWS)
        d_skip = d_skip + pair_sums(jnp.sum(dy_at * x, axis=0, keepdims=True), j, 1)
    dact[:, 384:512] = db[...] + mm(weighted[...], carry_low)
    dact[:, 512:640] = dc[...]
    d_cum = d_cum - d_tail
    d_decay = jnp.zeros((1, 128), F32)
    lane = iota((1, 128), 1)
    for h in range(6):
        hs = slice(64 * h, 64 * h + 64)
        d_decay = d_decay + jnp.where(lane == h, jnp.sum(carry[hs, :] * state[hs, :]), 0.0)
    d_last = (
        jnp.sum(d_tail, axis=0, keepdims=True)
        + d_decay * jnp.exp(last) * colp[ROWS - 1 : ROWS, 1:2]
    )
    later = iota((ROWS, ROWS), 0) <= iota((ROWS, ROWS), 1)
    d_log = d_last + jnp.dot(
        later.astype(F32), d_cum, precision=HIGHEST, preferred_element_type=F32
    )
    rate = -jnp.exp(heads[1:2, :])
    d_step = d_step + rate * d_log
    raw = proj[:, STEP:WIDTH] + heads[0:1, :]
    real = iota((ROWS, 128), 1) < 6
    d_raw = jnp.where(real, d_step * sigmoid(raw), 0.0)
    dstep_o[...] = d_raw.astype(BF16)
    small_o[...] = jnp.zeros((32, 128), F32)
    sums = (
        jnp.sum(d_raw, axis=0, keepdims=True),
        jnp.sum(d_log * rate * step, axis=0, keepdims=True),
        d_skip,
    )
    for n, value in enumerate(sums):
        high = value.astype(BF16).astype(F32)
        small_o[20 + n : 21 + n, :] = high
        small_o[23 + n : 24 + n, :] = value - high
    fill_extended(proj, near, ext)
    sig = sigmoid(pre[...])
    d_pre = dact[...] * sig * (1.0 + pre[...] * (1.0 - sig))
    dext[...] = jnp.zeros((8 + ROWS, CONV), F32)
    for k in range(4):
        kept = d_pre * colp[:, 2 + k : 3 + k]
        rows = slice(5 + k, 5 + k + ROWS)
        taps = jnp.sum(ext[rows, :] * kept, axis=0, keepdims=True)
        for j in range(5):
            small_o[5 * k + j : 5 * k + j + 1, :] = taps[:, 128 * j : 128 * j + 128]
        dext[rows, :] = dext[rows, :] + kept * kern[k : k + 1, :]
    rim_o[...] = dext[0:8, :]
    dconv_o[...] = dext[8 : 8 + ROWS, :]


def feed_forward_back_kernel(
    core, own, other, gate_up, w_gu, w_down, normed, gain,
    grad_o, d_gu_o, mine_o, other_o, prod_o, full,
):
    place_halves(core, own, other, grad_o)
    d_swiglu = mm(grad_o[...], w_down[...])
    units = d_swiglu.shape[1]
    gate = gate_up[:, 0:units]
    up = gate_up[:, units : 2 * units]
    sig = sigmoid(gate)
    d_gu_o[:, 0:units] = (d_swiglu * up * sig * (1.0 + gate * (1.0 - sig))).astype(BF16)
    d_gu_o[:, units : 2 * units] = (d_swiglu * gate * sig).astype(BF16)
    part = mm_t(d_gu_o[...], w_gu[...])
    full[...] = part
    deal_halves(core, full, mine_o, other_o)
    prod_o[...] = (part * normed[...].astype(F32) / gain[...]).astype(BF16)


def normed_back_kernel(
    core, dgate, dq, dconv, rim, dkv, k1, k2, k3, dstep, w_gate, w_q, w_inner, w_bc, w_kv, w_dt,
    normed, gain, cos, sin,
    late_o, mine_o, other_o, prod_o, full,
):
    late_o[0 : ROWS - 16, 0:CONV] = dconv[0 : ROWS - 16, :].astype(BF16)
    end = dconv[ROWS - 16 : ROWS, :]
    end = end + jnp.concatenate([jnp.zeros((8, CONV), F32), rim[...]], axis=0)
    late_o[ROWS - 16 : ROWS, 0:CONV] = end.astype(BF16)
    kv = dkv[...]
    for k in (k1, k2, k3):
        kv = kv + k[0:ROWS, :].astype(F32)
    is_key = iota((ROWS, 128), 1) < 64
    kv = jnp.where(is_key, turn(kv, cos[...], -sin[...]), kv)
    late_o[:, CONV : CONV + 128] = kv.astype(BF16)
    part = (
        mm_t(dgate[...], w_gate[...])
        + mm_t(dq[...], w_q[...])
        + mm_t(late_o[:, 0:384], w_inner[...])
        + mm_t(late_o[:, 384:640], w_bc[...])
        + mm_t(late_o[:, 640:768], w_kv[...])
        + mm_t(dstep[...], w_dt[...])
    )
    full[...] = part
    deal_halves(core, full, mine_o, other_o)
    prod_o[...] = (part * normed[...].astype(F32) / gain[...]).astype(BF16)


def row_block(segment, left, extra, at):
    rows = pl.ds(pl.multiple_of(at * 128, 128), 128)
    total = None
    for i, right in segment[0]:
        term = t_mm(left[i][:, rows], right[...])
        total = term if total is None else total + term
    if segment[1]:
        total = jnp.concatenate([extra[...]] * 4, axis=0)
    return total


class Reduction:
    def __init__(self, left, segments, extra=None):
        self.left, self.extra = list(left), extra
        self.terms = [[i for i, _ in seg] for seg in segments]
        self.rights = [r for seg in segments for _, r in seg]
        self.widths = [seg[0][1].shape[1] for seg in segments]
        if extra is not None:
            self.terms.append([])
            self.widths.append(128)
        self.columns = sum(self.widths)
        self.z = (lax.axis_index("dp") % 4).astype(jnp.int32).reshape(1)

    def run(self, kernel, outs, more=(), scratch=(), after=()):
        args = [self.z, *self.left, *self.rights]
        args += [] if self.extra is None else [self.extra]
        count, n_more = len(args), len(more)

        def inner(*refs):
            z, rest = refs[0], refs[1:count]
            left = rest[: len(self.left)]
            rights = list(rest[len(self.left) : len(self.left) + len(self.rights)])
            extra = rest[-1] if self.extra is not None else None
            segments, at = [], 0
            for n, (terms, width) in enumerate(zip(self.terms, self.widths)):
                pairs = [(i, rights.pop(0)) for i in terms]
                last = extra is not None and n == len(self.terms) - 1
                segments.append(((pairs, last), slice(at, at + width)))
                at += width

            def block(dp_hi, offset, columns_done):
                place = dp_hi * 4 + (z[0] + offset) % 4
                for segment, columns in segments:
                    columns_done(columns, row_block(segment, left, extra, place))

            kernel(block, refs[count : count + n_more], refs[count + n_more :])

        return call(inner, outs, (*args, *more), scratch, after)

    def ring(self, x, k):
        route = [(d, (d // 4) * 4 + (d + k) % 4) for d in range(8)]
        return lax.ppermute(x, "dp", route)

    def first(self):
        def kernel(block, _, outs):
            def into(out, rows):
                def done(columns, value):
                    out[rows, columns] = value.astype(BF16)

                return done

            for dp_hi in range(2):
                block(dp_hi, 2, into(outs[dp_hi], slice(0, 128)))
                rows = slice(128 * dp_hi, 128 * dp_hi + 128)
                for offset, out in ((1, outs[2]), (3, outs[3]), (0, outs[4])):
                    block(dp_hi, offset, into(out, rows))

        halves, blocks = ((128, self.columns), BF16), ((256, self.columns), BF16)
        sent = self.run(kernel, [halves] * 2 + [blocks] * 3)
        self.got = (self.ring(sent[0], 1), self.ring(sent[1], -1))
        self.ahead, self.behind, self.own = sent[2:]
        return [sent[4]]

    def second(self):
        low = (self.ahead[:128].astype(F32) + self.got[0].astype(F32)).astype(BF16)
        high = (self.behind[128:].astype(F32) + self.got[1].astype(F32)).astype(BF16)
        ahead = jnp.concatenate([low, self.ahead[128:]], axis=0)
        behind = jnp.concatenate([self.behind[:128], high], axis=0)
        self.got = (self.ring(ahead, 1), self.ring(behind, -1))
        return [ahead, behind]

    def third(self):
        ctx = lax.axis_index("ctx").astype(jnp.int32).reshape(1)

        def kernel(ctx, own, one, two, *refs):
            outs, total = refs[:4], refs[4]
            total[...] = own[...].astype(F32) + (one[...].astype(F32) + two[...].astype(F32))
            for k in range(4):
                for dp_hi in range(2):
                    start = 128 * dp_hi + 32 * ((ctx[0] + k) % 4)
                    piece = total[pl.ds(pl.multiple_of(start, 32), 32), :]
                    outs[k][32 * dp_hi : 32 * dp_hi + 32, :] = piece.astype(BF16)

        outs = call(
            kernel, [((64, self.columns), BF16)] * 4, (ctx, self.own, *self.got),
            [pltpu.VMEM((256, self.columns), F32)],
        )
        routes = [[(i, (i + k) % 4) for i in range(4)] for k in range(4)]
        self.got = [outs[0]] + [lax.ppermute(outs[k], "ctx", routes[k]) for k in (1, 2, 3)]
        return list(outs[1:])

    def fourth(self):
        dp_hi = lax.axis_index("dp") // 4
        total = sum(g.astype(F32) for g in self.got).reshape(2, 32, self.columns)
        mine = lax.dynamic_index_in_dim(total, dp_hi, 0, False)
        other = lax.dynamic_index_in_dim(total, 1 - dp_hi, 0, False).astype(BF16)
        self.got = mine + lax.ppermute(other, "dp", [(d, d ^ 4) for d in range(8)]).astype(F32)
        return [other]


def rms_scale(x):
    return lax.rsqrt(jnp.mean(x * x, axis=-1, keepdims=True) + EPSILON)


def body(
    hidden_in, segments, cotangent, norm_attn, w_zx, w_dt, w_bc, conv_x, conv_bc, dt_bias,
    a_log, d_skip, w_q, w_kv, w_o, w_out, norm_ffn, w_gu, w_down,
):
    layers, width = norm_attn.shape
    rows = hidden_in.shape[1]
    ctx = lax.axis_index("ctx")
    tensor = lax.axis_index("tensor")
    seg_row = segments[0]
    start = ctx * rows
    seg_pad = jnp.concatenate([jnp.full((3 * rows,), -1, jnp.int32), seg_row])
    windows = [
        lax.dynamic_slice_in_dim(seg_pad, start + (3 - k) * rows, rows) for k in range(4)
    ]
    here = windows[0]
    segr = jnp.concatenate(windows).astype(F32)[None]
    near = lax.dynamic_slice_in_dim(seg_pad, start + 3 * rows - 3, rows + 3)
    columns = [here.astype(F32), (here == near[2]).astype(F32)]
    columns += [(near[k : k + rows] == here).astype(F32) for k in range(4)]
    columns += [(here == here[-1]).astype(F32)]
    colp = jnp.pad(jnp.stack(columns, axis=1), ((0, 0), (0, 121)))
    positions = (start + jnp.arange(rows)).astype(F32)
    lane = jnp.arange(128) % 32
    frequency = jnp.exp(-jnp.log(10000.0) * lane.astype(F32) * (2.0 / HD))
    angles = positions[:, None] * frequency[None]
    cos, sin = jnp.cos(angles), jnp.sin(angles)
    kv_head = tensor // 2
    units = w_down.shape[2]

    saved = []
    core = (tensor & 1).astype(jnp.int32).reshape(1)
    half_bf, half_f = ((rows // 2, width), BF16), ((rows // 2, width), F32)
    full_rows = [pltpu.VMEM((rows, width), F32)]
    kernels = jnp.swapaxes(jnp.concatenate([conv_x, conv_bc], axis=1).astype(F32), 1, 2)
    w_dt_wide = jnp.pad(w_dt, ((0, 0), (0, 0), (0, 122)))
    full = hidden_in[0].astype(F32)
    resid = own_half(full)
    for l in range(layers):
        kv_w = lax.dynamic_slice_in_dim(w_kv[l], kv_head * HD, HD, axis=2).reshape(width, 2 * HD)
        w_zx_l, w_gu_l = w_zx[l], w_gu[l]
        if l > 0:
            w_zx_l, w_gu_l, _ = lax.optimization_barrier((w_zx_l, w_gu_l, saved[0]["proj"]))
        w_in = (
            w_zx_l[:, 0], Far(w_q, l), w_zx_l[:, 1], Far(w_bc, l), kv_w, Far(w_dt_wide, l)
        )
        gate_up_w = w_gu_l.reshape(width, -1)
        kern = Far(kernels, l)
        heads = jnp.pad(
            jnp.stack([dt_bias[l], a_log[l], d_skip[l]]), ((0, 5), (0, 122))
        )
        gain_attn = norm_attn[l].astype(F32)[None]
        gain_ffn = norm_ffn[l].astype(F32)[None]
        if l == 0:
            normed = (full * rms_scale(full) * gain_attn).astype(BF16)
            halves = normed.reshape(2, rows // 2, width)
            parts = [lax.dynamic_index_in_dim(halves, i, 0, False) for i in (core[0], 1 - core[0])]
            halves = (core, *parts)
        else:
            halves = both_halves(low)
        normed, proj, q, kv, rim = call(
            project_kernel,
            [((rows, width), BF16), ((rows, WIDTH), F32), ((rows, 128), BF16),
             ((rows, 128), BF16), ((80, 128), BF16)],
            (*halves, *w_in, cos, sin),
        )
        rim = shifted(rim, "ctx", 1)
        pre, yloc, stepcum, msg = call(
            ssm_local_kernel,
            [((rows, CONV), F32), ((rows, 384), F32), ((rows, 256), F32), ((MESSAGE, 128), BF16)],
            (proj, rim, kv, kern, heads, colp, segr),
            [pltpu.VMEM((8 + ROWS, CONV), F32)],
        )
        states = [shifted(msg, "ctx", k) for k in (1, 2, 3)]
        kvs = (msg, *states)
        (att,) = call(attention_kernel, [((rows, 128), BF16)], (q, *kvs, colp, segr))
        state, y, feat, *mixer = call(
            mixer_kernel,
            [((384, 128), F32), ((rows, 384), F32), ((rows, 512), BF16), half_bf, half_bf],
            (core, proj, pre, yloc, stepcum, *states, heads, colp, att, Far(w_o, l), Far(w_out, l)),
            full_rows,
        )
        hidden, low = call(
            normalise_kernel, [half_f, half_bf], (*chip_sums(*mixer), resid, gain_ffn)
        )
        normed_ffn, gate_up, swiglu, *ffn = call(
            feed_forward_kernel,
            [((rows, width), BF16), ((rows, 2 * units), F32), ((rows, units), BF16),
             half_bf, half_bf],
            (*both_halves(low), gate_up_w, Far(w_down, l)),
            full_rows,
        )
        saved.append(
            dict(
                w_in=w_in, gate_up_w=gate_up_w, kern=kern, heads=heads, gain_attn=gain_attn,
                gain_ffn=gain_ffn, resid=resid, normed=normed, proj=proj, q=q, kvs=kvs, rim=rim,
                pre=pre, stepcum=stepcum, state=state, y=y, feat=feat, hidden=hidden,
                normed_ffn=normed_ffn, gate_up=gate_up, swiglu=swiglu,
            )
        )
        if l + 1 < layers:
            resid, low = call(
                normalise_kernel, [half_f, half_bf],
                (*chip_sums(*ffn), hidden, norm_attn[l + 1].astype(F32)[None]),
            )
    one, two = chip_sums(*ffn)
    out = gather_half((hidden + (one.astype(F32) + two.astype(F32))).astype(BF16))

    grad = own_half(cotangent[0])
    grad_low = grad.astype(BF16)
    lane = jnp.arange(128)
    hot = [jnp.broadcast_to((lane == n).astype(BF16), (rows, 128)) for n in (6, 7)]
    owned = [None] * layers
    pins = []
    for l in reversed(range(layers)):
        s = saved[l]
        grad_ffn, d_gu, *part, prod_ffn = call(
            feed_forward_back_kernel,
            [((rows, width), BF16), ((rows, 2 * units), BF16), half_bf, half_bf,
             ((rows, width), BF16)],
            (*both_halves(grad_low), Far(s["gate_up"]), Far(s["gate_up_w"]), Far(w_down, l),
             Far(s["normed_ffn"]), s["gain_ffn"]),
            full_rows,
            pins,
        )
        group_ffn = Reduction(
            (Far(s["normed_ffn"]), grad_ffn), [[(0, d_gu)], [(1, Far(s["swiglu"]))]]
        )
        pins = group_ffn.first()
        grad_hidden, low = call(
            normalise_back_kernel, [half_f, half_bf],
            (*chip_sums(*part), Far(s["hidden"]), s["gain_ffn"], grad),
        )
        gm, datt, dgate, dy, dc, msg = call(
            finish_back_kernel,
            [
                ((rows, width), BF16), ((rows, 128), BF16), ((rows, 384), BF16),
                ((rows, 384), BF16), ((rows, 128), F32), ((400, 128), BF16),
            ],
            (*both_halves(low), Far(w_o, l), Far(w_out, l), Far(s["proj"]),
             Far(s["pre"]), Far(s["y"]), Far(s["stepcum"]), Far(s["state"]), Far(s["heads"]), Far(colp)),
            [pltpu.VMEM((ROWS, 384), BF16)],
            pins,
        )
        dq, dkv_own, *sents = call(
            attention_back_kernel,
            [((rows, 128), BF16), ((rows, 128), F32)] + [((MESSAGE, 128), BF16)] * 3,
            (Far(s["q"]), *(Far(k) for k in s["kvs"]), Far(colp), Far(segr), datt, Far(cos), Far(sin), msg),
        )
        carries = [shifted(sents[k - 1], "ctx", -k) for k in (1, 2, 3)]
        group_mid = Reduction(
            (Far(s["normed"]), gm), [[(0, dgate)], [(0, dq)], [(1, Far(s["feat"]))]]
        )
        if l < layers - 1:
            pins = group_ffn_up.fourth() + group_mid_up.third() + group_late.second()
        else:
            pins = group_ffn.second() + group_mid.first()
        dxs, db, dc = call(
            ssm_back_kernel,
            [((rows, 384), F32), ((rows, 128), F32), ((rows, 128), F32)],
            (Far(s["pre"]), Far(s["stepcum"]), dy, dc, Far(colp), Far(segr)),
        )
        dconv, rim, dstep, small = call(
            conv_back_kernel,
            [((rows, CONV), F32), ((8, CONV), F32), ((rows, 128), BF16), ((32, 128), F32)],
            (Far(s["proj"]), Far(s["rim"]), s["kern"], Far(s["heads"]), Far(colp), Far(s["pre"]),
             Far(s["stepcum"]), dy, Far(s["y"]), dxs, db, dc, Far(s["state"]), *carries),
            [
                pltpu.VMEM((384, 128), F32), pltpu.VMEM((ROWS, 384), BF16),
                pltpu.VMEM((ROWS, CONV), F32), pltpu.VMEM((8 + ROWS, CONV), F32),
                pltpu.VMEM((8 + ROWS, CONV), F32),
            ],
            pins,
        )
        pins = []
        if l < layers - 1:
            pins = group_ffn.second() + group_mid.first()
            pins += group_mid_up.fourth() + group_late.third()
        extra = small
        rim_got = shifted(rim, "ctx", -1)
        late, *part, prod_attn = call(
            normed_back_kernel,
            [((rows, 768), BF16), half_bf, half_bf, ((rows, width), BF16)],
            (core, dgate, dq, dconv, rim_got, dkv_own, *carries, dstep, *s["w_in"], Far(s["normed"]),
             s["gain_attn"], Far(cos), Far(sin)),
            full_rows,
            pins,
        )
        late_cols = [
            [(0, late)],
            [(0, dstep), (1, hot[0]), (2, hot[1])],
        ]
        mix_left = (Far(s["normed"]), prod_attn, prod_ffn)
        if l > 0:
            group_late = Reduction(mix_left, late_cols, extra)
            pins = group_ffn.third() + group_mid.second() + group_late.first()
            group_ffn_up, group_mid_up = group_ffn, group_mid
            owned[l] = (group_ffn, group_mid, group_late)
        else:
            late_up = group_late
            group_late = Reduction(mix_left, late_cols, extra)
            group_late.first()
            late_up.fourth()
            group_mid.second()
            group_ffn.third()
            group_late.second()
            group_mid.third()
            group_ffn.fourth()
            group_late.third()
            group_mid.fourth()
            group_late.fourth()
            owned[l] = (group_ffn, group_mid, group_late)
        grad, grad_low = call(
            normalise_back_kernel, [half_f, half_bf],
            (*chip_sums(*part), Far(s["resid"]), s["gain_attn"], grad_hidden),
        )
    grad_hidden_in = gather_half(grad)

    everything = jnp.stack([jnp.concatenate([g.got for g in o], axis=1) for o in owned])
    ffn, mid, late = everything[..., :1536], everything[..., 1536:2560], everything[..., 2560:]
    tile = late[:, :, 896:]
    taps = tile[:, :20].reshape(layers, 4, CONV)
    sums = (tile[:, 20:23] + tile[:, 23:26])[..., :6]
    index = lax.axis_index("dp") * 4 + ctx
    state = lax.dynamic_slice_in_dim(taps[..., 384:], index * 8, 8, 2)
    state = jnp.pad(jnp.swapaxes(state, 1, 2).reshape(layers, 32, 1), ((0, 0), (0, 0), (0, 119)))
    shared = jnp.concatenate([late[:, :, 384:776], state], axis=2)
    shared = jnp.moveaxis(shared.reshape(layers, 4, -1, 512), 1, 0)
    shared = lax.all_to_all(shared, "tensor", 0, 0, tiled=True)
    total = jnp.sum(shared, axis=0)
    head_kv = [jnp.sum(shared[2 * k : 2 * k + 2, ..., 256:384], axis=0) for k in range(2)]
    head_kv = [h.reshape(*h.shape[:-1], 2, HD) for h in head_kv]
    return (
        out[None],
        grad_hidden_in[None],
        total[..., 390],
        jnp.stack([mid[..., :384], late[..., :384]], axis=2),
        late[..., 768:774],
        total[..., :256],
        jnp.swapaxes(taps[..., :384], 1, 2),
        total[..., 392].reshape(layers, 2, 4),
        sums[:, 0],
        sums[:, 1],
        sums[:, 2],
        mid[..., 384:512],
        jnp.concatenate(head_kv, axis=-1),
        mid[..., 512:640],
        mid[..., 640:1024],
        total[..., 391],
        ffn[..., : 2 * units].reshape(layers, -1, 2, units),
        ffn[..., 2 * units :],
    )


def solution(mesh):
    placed = (
        P("dp", "ctx", None),
        P("dp", None),
        P("dp", "ctx", None),
        P(),
        P(None, None, None, "tensor"),
        P(None, None, "tensor"),
        P(),
        P(None, "tensor", None),
        P(),
        P(None, "tensor"),
        P(None, "tensor"),
        P(None, "tensor"),
        P(None, None, "tensor"),
        P(),
        P(None, None, "tensor"),
        P(None, None, "tensor"),
        P(),
        P(None, None, None, "tensor"),
        P(None, None, "tensor"),
    )
    return jax.shard_map(
        body,
        mesh=mesh,
        in_specs=placed,
        out_specs=(
            P("dp", "ctx", None),
            P("dp", "ctx", None),
            P(None, ("dp", "ctx", "tensor")),
            P(None, ("dp", "ctx"), None, "tensor"),
            P(None, ("dp", "ctx"), "tensor"),
            P(None, ("dp", "ctx", "tensor"), None),
            P(None, "tensor", None),
            P(None, ("dp", "ctx", "tensor"), None),
            P(None, "tensor"),
            P(None, "tensor"),
            P(None, "tensor"),
            P(None, ("dp", "ctx"), "tensor"),
            P(None, ("dp", "ctx", "tensor"), None, None),
            P(None, ("dp", "ctx"), "tensor"),
            P(None, ("dp", "ctx"), "tensor"),
            P(None, ("dp", "ctx", "tensor")),
            P(None, ("dp", "ctx"), None, "tensor"),
            P(None, ("dp", "ctx"), "tensor"),
        ),
        check_vma=False,
    )
```
